512 devices in a mesh: dp: 32 (over x, z_lo, core), ctx: 16 (over y, z_hi).
Axes of the slice: x: 4, y: 8, z: 8 (z_hi: 2, z_lo: 4; z = z_hi * 4 + z_lo), core: 2. Of those that a mesh axis runs over, the one named last changes fastest.
Arguments:
- query_raw: bfloat16 [32, 2048, 1024], P('dp', 'ctx'), may hold values from -40 to 40
- key_raw: bfloat16 [32, 2048, 128], P('dp', 'ctx'), may hold values from -40 to 40
- values: bfloat16 [32, 2048, 128], P('dp', 'ctx'), may hold values from -6 to 6
- out_grad: bfloat16 [32, 2048, 1024], P('dp', 'ctx'), may hold values from -6 to 6
- doc_lengths: int32 [32, 32], P('dp'), may hold values from 0 to 2048, as said below
- query_gain: float32 [128], replicated, may hold values from 0.5 to 5.5
- key_gain: float32 [128], replicated, may hold values from 0.5 to 5.5
Outputs:
- output: bfloat16 [32, 2048, 1024], P('dp', 'ctx')
- query_raw_grad: bfloat16 [32, 2048, 1024], P('dp', 'ctx')
- key_raw_grad: bfloat16 [32, 2048, 128], P('dp', 'ctx')
- values_grad: bfloat16 [32, 2048, 128], P('dp', 'ctx')
- query_gain_grad: float32 [128], replicated
- key_gain_grad: float32 [128], replicated
The draws below stay inside these ranges and needn't reach their ends.
Inputs may be any that keep to these rules, and one draw needn't show every extreme that they name: `doc_lengths`: the lengths of each micro-batch sum to 2048; entries that are 0 come after all nonzero ones.
All inputs are finite; a program needn't handle non-finite values.
Results may differ from the reference program's by a relative error of at most 0.03.
The reference program's roundings to bfloat16 on the way (of `queries`, `key_rows`, `weights` and `score_grad`) count: a program that leaves them out, or rounds other values in their place, can miss the bound.
Values may be sent and summed in bfloat16 or wider, within the bound.
No kernel may reach another device: no remote copies, remote signals or barrier semaphores. Data moves between devices by JAX's collectives and lax.ppermute only.
A program may use at most 128 MiB of HBM per device.

```python
import math
import jax
import jax.numpy as jnp
from jax import lax

HEAD_DIM = 128
HEADS = 8
MAXDOCS = 32
SEQ = 2048
BATCH = 32
QW = 1024


def shared_keys(key, lower_scale, upper_scale):
    gauss = jax.random.normal(jax.random.fold_in(key, 101), (BATCH, SEQ, HEAD_DIM), jnp.float32)
    spread = jax.random.uniform(jax.random.fold_in(key, 102), (BATCH, SEQ, 1), jnp.float32, math.log(lower_scale), math.log(upper_scale))
    return gauss * jnp.exp(spread)


def draw_key_raw(key, part):
    key_values = shared_keys(key, 0.3, 3.0)
    return jnp.clip(key_values, -40.0, 40.0).astype(jnp.bfloat16)


def draw_query_raw(key, part):
    own_key = jax.random.fold_in(key, 7)
    gauss = jax.random.normal(jax.random.fold_in(own_key, 1), (BATCH, SEQ, HEADS, HEAD_DIM), jnp.float32)
    spread = jax.random.uniform(jax.random.fold_in(own_key, 2), (BATCH, SEQ, HEADS, 1), jnp.float32, math.log(0.3), math.log(3.0))
    noise = gauss * jnp.exp(spread)
    return jnp.clip(noise, -40.0, 40.0).reshape(BATCH, SEQ, HEADS * HEAD_DIM).astype(jnp.bfloat16)


def draw_query_gain(key, part):
    key = jax.random.fold_in(key, 21)
    lower_bound = 0.5
    upper_bound = 2.0
    return jnp.exp(jax.random.uniform(key, (HEAD_DIM,), jnp.float32, math.log(lower_bound), math.log(upper_bound)))


def draw_key_gain(key, part):
    key = jax.random.fold_in(key, 22)
    lower_bound = 0.5
    upper_bound = 2.0
    return jnp.exp(jax.random.uniform(key, (HEAD_DIM,), jnp.float32, math.log(lower_bound), math.log(upper_bound)))


def draw_doc_lengths(key, part):
    key = jax.random.fold_in(key, 31)
    order_key = jax.random.fold_in(key, 1)
    length_key = jax.random.fold_in(key, 2)
    place_key = jax.random.fold_in(key, 3)
    level = jax.random.permutation(order_key, BATCH) % 4
    longest = (SEQ // jnp.power(2, level)).astype(jnp.int32)
    lower_len = (longest // 2)[:, None]
    upper_len = longest[:, None] + 1
    raw_lengths = jax.random.randint(length_key, (BATCH, MAXDOCS), lower_len, upper_len).astype(jnp.int32)
    place = jnp.where(level == 0, 0, jax.random.randint(place_key, (BATCH,), 0, 4)).astype(jnp.int32)
    column = jnp.arange(MAXDOCS, dtype=jnp.int32)
    raw_lengths = jnp.where(column[None, :] == place[:, None], longest[:, None], raw_lengths)
    doc_ends = jnp.cumsum(raw_lengths, axis=1).astype(jnp.int32)
    before = doc_ends - raw_lengths
    return jnp.clip(SEQ - before, 0, raw_lengths).astype(jnp.int32)


def level_of(rng, shape, pieces, low, top_value):
    def one(dim, blocks):
        draws = jax.random.uniform(jax.random.fold_in(jax.random.fold_in(rng, 6), dim), (blocks,), jnp.float32, low / len(pieces), top_value / len(pieces))
        return jnp.repeat(jnp.exp(draws), shape[dim] // blocks).reshape((-1,) + (1,) * (len(shape) - dim - 1))

    gain = one(*pieces[0])
    for cut in pieces[1:]:
        gain = gain * one(*cut)
    return gain


def bell_draw(stream_key, extent, deviation, most, shards=(), kind=jnp.bfloat16):
    entries = jax.random.normal(stream_key, extent, jnp.float32) * deviation
    if len(shards) > 0:
        entries = level_of(stream_key, extent, shards, -0.22, 0.18) * entries
    return jnp.clip(entries, min=-most, max=most).astype(kind)


def setup_inputs(seed: int = 0) -> dict:
    streams_of = jax.random.split(jax.random.key(seed), 8)
    return {
        "query_raw": draw_query_raw(jax.random.fold_in(streams_of[7], 71), 0),
        "key_raw": draw_key_raw(jax.random.fold_in(streams_of[7], 71), 0),
        "values": bell_draw(streams_of[2], (BATCH, SEQ, HEAD_DIM), 1.0, 6.0, ((0, 32), (1, 16))),
        "out_grad": bell_draw(streams_of[3], (BATCH, SEQ, QW), 1.0, 6.0, ((0, 32), (1, 16))),
        "doc_lengths": draw_doc_lengths(jax.random.fold_in(streams_of[7], 71), 0),
        "query_gain": draw_query_gain(jax.random.fold_in(streams_of[7], 71), 0),
        "key_gain": draw_key_gain(jax.random.fold_in(streams_of[7], 71), 0),
    }


rope_theta = 1000000.0
norm_epsilon = 1e-06
masked_value = -1e+30

def rope_tables(positions, head_width):
    half_width = head_width // 2
    exponent = jnp.arange(half_width, dtype=jnp.float32) * (2.0 / head_width)
    frequency = jnp.power(jnp.float32(rope_theta), -exponent)
    angles = positions.astype(jnp.float32)[:, None] * frequency[None, :]
    return (jnp.cos(angles), jnp.sin(angles))

def rotate(vector, cosine, sine_table):
    half_width = vector.shape[-1] // 2
    lower_half = vector[..., :half_width]
    upper_half = vector[..., half_width:]
    return jnp.concatenate([lower_half * cosine - upper_half * sine_table, upper_half * cosine + lower_half * sine_table], axis=-1)

def normalize(raw_rows, gain_vector):
    as_float = raw_rows.astype(jnp.float32)
    inverse = lax.rsqrt(lax.optimization_barrier(jnp.mean(as_float * as_float, axis=-1, keepdims=True)) + norm_epsilon)
    unit_rows = as_float * inverse
    return (unit_rows * gain_vector, unit_rows, inverse)

def norm_back(upstream, unit_rows, inverse, gain_vector):
    scaled = upstream * gain_vector
    return inverse * (scaled - unit_rows * lax.optimization_barrier(jnp.mean(scaled * unit_rows, axis=-1, keepdims=True)))

def token_starts(doc_ends, first_token, tok_count):
    tokens = first_token + jnp.arange(tok_count, dtype=jnp.int32)
    before = doc_ends[None, :] <= tokens[:, None]
    return lax.optimization_barrier(jnp.max(jnp.where(before, doc_ends[None, :], 0), axis=1)).astype(jnp.int32)

def single_batch(query_raw, key_raw, values, out_grad, doc_lengths, query_gain, key_gain):
    score_scale = HEAD_DIM ** (-0.5)
    doc_ends = jnp.cumsum(doc_lengths).astype(jnp.int32)
    doc_starts = token_starts(doc_ends, 0, SEQ)
    positions = jnp.arange(SEQ, dtype=jnp.int32) - doc_starts
    cosine, sine_table = rope_tables(positions, HEAD_DIM)
    query_normed, query_unit, query_inverse = normalize(query_raw.reshape(SEQ, HEADS, HEAD_DIM), query_gain)
    queries = rotate(query_normed, cosine[:, None, :], sine_table[:, None, :]).astype(jnp.bfloat16)
    key_normed, key_unit, key_inverse = normalize(key_raw, key_gain)
    key_rows = rotate(key_normed, cosine, sine_table).astype(jnp.bfloat16)
    query_rows = queries.reshape(SEQ * HEADS, HEAD_DIM)
    grad_rows = out_grad.reshape(SEQ * HEADS, HEAD_DIM)
    row_token = jnp.arange(SEQ * HEADS, dtype=jnp.int32) // HEADS
    row_start = jnp.repeat(doc_starts, HEADS)
    columns = jnp.arange(SEQ, dtype=jnp.int32)
    allowed = (columns[None, :] >= row_start[:, None]) & (columns[None, :] <= row_token[:, None])
    scores = jnp.dot(query_rows, key_rows.T, preferred_element_type=jnp.float32) * score_scale
    scores = jnp.where(allowed, scores, masked_value)
    row_max = lax.optimization_barrier(jnp.max(scores, axis=1, keepdims=True))
    row_sum = lax.optimization_barrier(jnp.sum(jnp.where(allowed, jnp.exp(scores - row_max), 0.0), axis=1, keepdims=True))
    log_total = row_max + jnp.log(row_sum)
    prob_tile = jnp.where(allowed, jnp.exp(scores - log_total), 0.0)
    weights = prob_tile.astype(jnp.bfloat16)
    output = jnp.dot(weights, values, preferred_element_type=jnp.float32).astype(jnp.bfloat16)
    row_delta = lax.optimization_barrier(jnp.sum(grad_rows.astype(jnp.float32) * output.astype(jnp.float32), axis=1, keepdims=True))
    prob_grad = jnp.dot(grad_rows, values.T, preferred_element_type=jnp.float32)
    score_grad = (prob_tile * (prob_grad - row_delta)).astype(jnp.bfloat16)
    query_grad = jnp.dot(score_grad, key_rows, preferred_element_type=jnp.float32) * score_scale
    key_grad = jnp.dot(score_grad.T, query_rows, preferred_element_type=jnp.float32) * score_scale
    values_grad = jnp.dot(weights.T, grad_rows, preferred_element_type=jnp.float32).astype(jnp.bfloat16)
    query_back = rotate(query_grad.reshape(SEQ, HEADS, HEAD_DIM), cosine[:, None, :], -sine_table[:, None, :])
    key_back = rotate(key_grad, cosine, -sine_table)
    query_raw_grad = norm_back(query_back, query_unit, query_inverse, query_gain).reshape(SEQ, QW).astype(jnp.bfloat16)
    key_raw_grad = norm_back(key_back, key_unit, key_inverse, key_gain).astype(jnp.bfloat16)
    query_gain_part = lax.optimization_barrier(jnp.sum(query_back * query_unit, axis=(0, 1)))
    key_gain_part = lax.optimization_barrier(jnp.sum(key_back * key_unit, axis=0))
    return (output.reshape(SEQ, QW), query_raw_grad, key_raw_grad, values_grad, query_gain_part, key_gain_part)

def reference(query_raw, key_raw, values, out_grad, doc_lengths, query_gain, key_gain):

    def one_item(items):
        return single_batch(items[0], items[1], items[2], items[3], items[4], query_gain, key_gain)
    results = lax.map(one_item, (query_raw, key_raw, values, out_grad, doc_lengths))
    return (results[0], results[1], results[2], results[3], lax.optimization_barrier(jnp.sum(results[4], axis=0)), lax.optimization_barrier(jnp.sum(results[5], axis=0)))
```

```python
import functools
import math

import jax
import jax.numpy as jnp
from jax import lax
from jax.experimental import pallas as pl
from jax.experimental.pallas import tpu as pltpu
from jax.sharding import PartitionSpec as P

rope_theta = 1000000.0
norm_epsilon = 1e-06
masked_value = -1e30
D = 128
F32 = jnp.float32
BF16 = jnp.bfloat16
VM = pl.BlockSpec(memory_space=pltpu.VMEM)
SM = pl.BlockSpec(memory_space=pltpu.SMEM)
SCALE = D ** (-0.5)
LOG2E = math.log2(math.e)
GAIN_ROWS = 16


def dot(a, b):
    return jnp.dot(a, b, preferred_element_type=F32)


def sin_cos(angle):
    turns = jnp.floor(angle * (2.0 / math.pi) + 0.5)
    r = angle - turns * 1.5703125
    r = r - turns * 4.837512969970703125e-4
    r = r - turns * 7.549789948768648e-8
    r2 = r * r
    s = r + r * r2 * (-1.6666654611e-1 + r2 * (8.3321608736e-3 + r2 * -1.9515295891e-4))
    c = 1.0 - 0.5 * r2 + r2 * r2 * (
        4.166664568298827e-2 + r2 * (-1.388731625493765e-3 + r2 * 2.443315711809948e-5)
    )
    quarter = turns.astype(jnp.int32)
    odd = (quarter & 1) == 1
    sin_part = jnp.where(odd, c, s)
    cos_part = jnp.where(odd, s, c)
    sin_part = jnp.where((quarter & 2) == 2, -sin_part, sin_part)
    cos_part = jnp.where(((quarter + 1) & 2) == 2, -cos_part, cos_part)
    return sin_part, cos_part


def starts_of(lengths, tokens):
    end = jnp.int32(0)
    start = jnp.zeros_like(tokens)
    for d in range(lengths.shape[1]):
        end = end + lengths[0, d]
        start = jnp.where(tokens >= end, end, start)
    return start


def rotate(x, cosine, sine):
    return x * cosine + pltpu.roll(x, D // 2, 1) * sine


def rotate_back(x, cosine, sine):
    return x * cosine - pltpu.roll(x, D // 2, 1) * sine


def unit_of(raw):
    x = raw.astype(F32)
    inverse = lax.rsqrt(jnp.mean(x * x, axis=1, keepdims=True) + norm_epsilon)
    return x * inverse, inverse


def prep_kernel(
    heads, token_ref, lengths, freq, q_raw, dout, q_gain,
    cos_ref, sin_ref, cos_own, sin_own, q_ref, qt_ref, do_ref, dot_ref, pos_ref,
):
    tokens_own = q_raw.shape[0]
    seq = cos_ref.shape[0]
    row = lax.broadcasted_iota(jnp.int32, (D, D), 0)
    lane = lax.broadcasted_iota(jnp.int32, (D, D), 1)
    tokens = row * D + lane
    positions = tokens - starts_of(lengths, tokens)
    pos_ref[...] = positions.astype(F32).T
    first_lanes = lane < D // 2
    for i in range(seq // D):
        angle = pos_ref[:, i : i + 1] * freq[...]
        s, c = sin_cos(angle)
        cos_ref[i * D : (i + 1) * D, :] = c
        sin_ref[i * D : (i + 1) * D, :] = jnp.where(first_lanes, -s, s)
    first = pl.multiple_of(token_ref[0], tokens_own)
    cosine = cos_ref[pl.ds(first, tokens_own), :]
    sine = sin_ref[pl.ds(first, tokens_own), :]
    cos_own[...] = cosine
    sin_own[...] = sine
    for h in range(heads):
        cols = slice(h * D, (h + 1) * D)
        rows = slice(h * tokens_own, (h + 1) * tokens_own)
        unit, _ = unit_of(q_raw[:, cols])
        q = rotate(unit * q_gain[...], cosine, sine)
        q_ref[rows, :] = q.astype(BF16)
        qt_ref[:, rows] = q.T.astype(BF16)
        g = dout[:, cols]
        do_ref[rows, :] = g
        dot_ref[:, rows] = g.astype(F32).T.astype(BF16)


def attend_kernel(
    heads, token_ref, lengths, kv, cos_ref, sin_ref, cos_own, sin_own, q_ref, qt_ref, do_ref, dot_ref,
    q_raw, q_gain, k_gain,
    out_ref, dq_ref, dkv_ref, gains_ref,
    s_buf, w_buf, k_buf, kt_buf, vt_buf, ot_buf, dqt_buf, max_buf, sum_buf, row_buf, kg_buf,
):
    blocks, kb, _ = kv.shape
    tokens_own = q_raw.shape[0]
    cols_all = heads * tokens_own
    cc = 2 * tokens_own
    chunks = cols_all // cc
    first = token_ref[0]
    end = jnp.int32(0)
    low = jnp.int32(0)
    for d in range(lengths.shape[1]):
        end = end + lengths[0, d]
        low = jnp.where(end <= first, end, low)
    lo = low // kb
    hi = (first + tokens_own - 1) // kb + 1
    tok = first + lax.broadcasted_iota(jnp.int32, (8, tokens_own), 1)
    start_row = starts_of(lengths, tok)[:1]
    tok_row = tok[:1]
    dkv_ref[...] = jnp.zeros_like(dkv_ref)
    max_buf[...] = jnp.full_like(max_buf, masked_value)
    sum_buf[...] = jnp.zeros_like(sum_buf)
    ot_buf[...] = jnp.zeros_like(ot_buf)
    dqt_buf[...] = jnp.zeros_like(dqt_buf)
    kg_buf[...] = jnp.zeros_like(kg_buf)
    factor = SCALE * LOG2E

    def block_rows(b):
        return pl.ds(pl.multiple_of(b * kb, kb), kb)

    def scores_step(b, carry):
        rows = block_rows(b)
        unit, _ = unit_of(kv[b, :, :D])
        k = rotate(unit * k_gain[...], cos_ref[rows, :], sin_ref[rows, :])
        k_rows = k.astype(BF16)
        k_buf[b] = k_rows
        kt_buf[b] = k.T.astype(BF16)
        vt_buf[b] = kv[b, :, D:].astype(F32).T.astype(BF16)
        key = b * kb + lax.broadcasted_iota(jnp.int32, (kb, tokens_own), 0)
        allowed = (key >= start_row) & (key <= tok_row)
        bias = jnp.where(allowed, 0.0, masked_value)
        for c in range(chunks):
            cs = slice(c * cc, (c + 1) * cc)
            s = dot(k_rows, qt_ref[:, cs]) * factor + jnp.concatenate([bias, bias], 1)
            s_buf[b, :, cs] = s
            max_buf[:, cs] = jnp.maximum(max_buf[:, cs], jnp.max(s.reshape(kb // 8, 8, cc), axis=0))
        return carry

    lax.fori_loop(lo, hi, scores_step, 0)
    row_buf[:1, :] = jnp.max(max_buf[...], axis=0, keepdims=True)

    def exp_step(b, carry):
        for c in range(chunks):
            cs = slice(c * cc, (c + 1) * cc)
            e = jnp.exp2(s_buf[b, :, cs] - row_buf[:1, cs])
            s_buf[b, :, cs] = e
            sum_buf[:, cs] += jnp.sum(e.reshape(kb // 8, 8, cc), axis=0)
        return carry

    lax.fori_loop(lo, hi, exp_step, 0)
    row_buf[:1, :] = 1.0 / jnp.sum(sum_buf[...], axis=0, keepdims=True)

    def values_step(b, carry):
        dv = jnp.zeros((kb, D), F32)
        for c in range(chunks):
            cs = slice(c * cc, (c + 1) * cc)
            prob = s_buf[b, :, cs] * row_buf[:1, cs]
            s_buf[b, :, cs] = prob
            w = prob.astype(BF16)
            ot_buf[:, cs] += dot(vt_buf[b], w)
            dv = dv + dot(w, do_ref[cs, :])
        dkv_ref[b, :kb, D:] = dv.astype(BF16)
        return carry

    lax.fori_loop(lo, hi, values_step, 0)
    for h in range(heads):
        hs = slice(h * tokens_own, (h + 1) * tokens_own)
        ot = ot_buf[:, hs].astype(BF16).astype(F32)
        out_ref[:, h * D : (h + 1) * D] = ot.T.astype(BF16)
        row_buf[:1, hs] = jnp.sum(ot * dot_ref[:, hs].astype(F32), axis=0, keepdims=True)

    def back_step(b, carry):
        rows = block_rows(b)
        dk = jnp.zeros((kb, D), F32)
        v_rows = kv[b, :, D:]
        for c in range(chunks):
            cs = slice(c * cc, (c + 1) * cc)
            dp = dot(v_rows, dot_ref[:, cs])
            ds = (s_buf[b, :, cs] * (dp - row_buf[:1, cs])).astype(BF16)
            dk = dk + dot(ds, q_ref[cs, :])
            dqt_buf[:, cs] += dot(kt_buf[b], ds)
        dk = dk * SCALE
        dkv_ref[b, :kb, :D] = dk.astype(BF16)
        unit, _ = unit_of(kv[b, :, :D])
        terms = rotate_back(dk, cos_ref[rows, :], sin_ref[rows, :]) * unit
        kg_buf[...] += jnp.sum(terms.reshape(kb // 8, 8, D), axis=0)
        return carry

    lax.fori_loop(lo, hi, back_step, 0)
    cosine = cos_own[...]
    sine = sin_own[...]
    q_sum = jnp.zeros((8, D), F32)
    for h in range(heads):
        hs = slice(h * tokens_own, (h + 1) * tokens_own)
        back = rotate_back(dqt_buf[:, hs].T * SCALE, cosine, sine)
        unit, inverse = unit_of(q_raw[:, h * D : (h + 1) * D])
        q_sum = q_sum + jnp.sum((back * unit).reshape(tokens_own // 8, 8, D), axis=0)
        scaled = back * q_gain[...]
        mean = jnp.mean(scaled * unit, axis=1, keepdims=True)
        dq_ref[:, h * D : (h + 1) * D] = (inverse * (scaled - unit * mean)).astype(BF16)
    gains_ref[:, :D] = jnp.broadcast_to(jnp.sum(q_sum, axis=0, keepdims=True), (8, D))
    gains_ref[:, D:] = jnp.broadcast_to(jnp.sum(kg_buf[...], axis=0, keepdims=True), (8, D))
    total = gains_ref[:1, :]
    high = total.astype(BF16).astype(F32)
    middle = (total - high).astype(BF16).astype(F32)
    lowest = total - high - middle
    row = lax.broadcasted_iota(jnp.int32, (GAIN_ROWS, 2 * D), 0)
    tail = jnp.where(row == 0, high, jnp.where(row == 1, middle, jnp.where(row == 2, lowest, 0.0)))
    for b in range(blocks):
        dkv_ref[b, kb:, :] = tail.astype(BF16)


def finish_kernel(own_ref, other_ref, k_raw, k_gain, cos_own, sin_own, dk_ref, dv_ref):
    total = own_ref[...] + other_ref[...].astype(F32)
    unit, inverse = unit_of(k_raw[...])
    back = rotate_back(total[:, :D], cos_own[...], sin_own[...])
    scaled = back * k_gain[...]
    mean = jnp.mean(scaled * unit, axis=1, keepdims=True)
    dk_ref[...] = (inverse * (scaled - unit * mean)).astype(BF16)
    dv_ref[...] = total[:, D:].astype(BF16)


def call_prep(token, lengths, freq, q_raw, dout, q_gain, seq, **kw):
    tokens_own, width = q_raw.shape
    heads = width // D
    rows = heads * tokens_own
    shapes = [
        ((seq, D), F32), ((seq, D), F32), ((tokens_own, D), F32), ((tokens_own, D), F32),
        ((rows, D), BF16), ((D, rows), BF16), ((rows, D), BF16), ((D, rows), BF16),
    ]
    return pl.pallas_call(
        functools.partial(prep_kernel, heads),
        out_shape=[jax.ShapeDtypeStruct(s, t) for s, t in shapes],
        in_specs=[SM, SM, VM, VM, VM, VM],
        out_specs=[VM] * len(shapes),
        scratch_shapes=[pltpu.VMEM((D, D), F32)],
        compiler_params=pltpu.CompilerParams(vmem_limit_bytes=32 * 2**20),
        cost_estimate=pl.CostEstimate(flops=40_000_000, bytes_accessed=4_000_000, transcendentals=0),
        name="prep",
        **kw,
    )(token, lengths, freq, q_raw, dout, q_gain)


def call_attend(token, lengths, kv, prepared, q_raw, q_gain, k_gain, **kw):
    tokens_own, width = q_raw.shape
    heads = width // D
    blocks, kb, _ = kv.shape
    rows = heads * tokens_own
    shapes = [
        ((tokens_own, width), BF16), ((tokens_own, width), BF16),
        ((blocks, kb + GAIN_ROWS, 2 * D), BF16), ((8, 2 * D), F32),
    ]
    scratch = [
        pltpu.VMEM((blocks, kb, rows), F32), pltpu.VMEM((8, 128), F32),
        pltpu.VMEM((blocks, kb, D), BF16), pltpu.VMEM((blocks, D, kb), BF16),
        pltpu.VMEM((blocks, D, kb), BF16), pltpu.VMEM((D, rows), F32), pltpu.VMEM((D, rows), F32),
        pltpu.VMEM((8, rows), F32), pltpu.VMEM((8, rows), F32), pltpu.VMEM((8, rows), F32),
        pltpu.VMEM((8, D), F32),
    ]
    return pl.pallas_call(
        functools.partial(attend_kernel, heads),
        out_shape=[jax.ShapeDtypeStruct(s, t) for s, t in shapes],
        in_specs=[SM, SM] + [VM] * 12,
        out_specs=[VM] * len(shapes),
        scratch_shapes=scratch,
        compiler_params=pltpu.CompilerParams(vmem_limit_bytes=40 * 2**20),
        cost_estimate=pl.CostEstimate(flops=3_200_000_000, bytes_accessed=8_000_000, transcendentals=2_000_000),
        name="attend",
        **kw,
    )(token, lengths, kv, *prepared, q_raw, q_gain, k_gain)


def call_finish(own, other, k_raw, k_gain, cos_own, sin_own, **kw):
    shape = jax.ShapeDtypeStruct(k_raw.shape, BF16)
    return pl.pallas_call(
        finish_kernel,
        out_shape=[shape, shape],
        in_specs=[VM] * 6,
        out_specs=[VM] * 2,
        name="finish",
        **kw,
    )(own, other, k_raw, k_gain, cos_own, sin_own)


def frequency_row():
    exponent = jnp.arange(D // 2, dtype=F32) * (2.0 / D)
    frequency = jnp.power(F32(rope_theta), -exponent)
    return jnp.concatenate([frequency, frequency])[None, :]


def sum_parts(received, kb):
    return jnp.sum(received[:, :kb].astype(F32), axis=0)


def body(query_raw, key_raw, values, out_grad, doc_lengths, query_gain, key_gain):
    tokens_own = query_raw.shape[1]
    ctx = lax.axis_size("ctx")
    dp = lax.axis_size("dp")
    seq = tokens_own * ctx
    kb = 2 * tokens_own
    half = ctx // 2
    me = lax.axis_index("ctx")
    side = me % 2
    token = (me * tokens_own)[None].astype(jnp.int32)
    q_gain = query_gain[None, :]
    k_gain = key_gain[None, :]
    columns = [[2 * y + z for y in range(half)] for z in range(2)]
    swap = [(i, i ^ 1) for i in range(ctx)]

    kv_own = jnp.concatenate([key_raw[0], values[0]], axis=1)
    kv_other = lax.ppermute(kv_own, "ctx", swap)
    prepared = call_prep(token, doc_lengths, frequency_row(), query_raw[0], out_grad[0], q_gain, seq)
    pair = jnp.where(
        side == 0,
        jnp.concatenate([kv_own, kv_other], axis=0),
        jnp.concatenate([kv_other, kv_own], axis=0),
    )
    kv = lax.all_to_all(
        jnp.broadcast_to(pair[None], (half, kb, 2 * D)), "ctx", 0, 0, axis_index_groups=columns
    )
    output, dq, dkv, _ = call_attend(
        token, doc_lengths, kv, prepared, query_raw[0], q_gain, k_gain
    )
    received = lax.all_to_all(dkv, "ctx", 0, 0, axis_index_groups=columns)
    summed = sum_parts(received, kb)
    gains = jnp.sum(received[:, kb : kb + 3].astype(F32), axis=(0, 1))
    own = lax.dynamic_slice_in_dim(summed, side * tokens_own, tokens_own, 0)
    theirs = lax.dynamic_slice_in_dim(summed, (1 - side) * tokens_own, tokens_own, 0)
    other = lax.ppermute(theirs.astype(BF16), "ctx", swap)
    groups = [
        [d * ctx + 2 * y + z for d in range(dp) for z in range(2)] for y in range(half)
    ]
    spread = lax.all_to_all(
        jnp.broadcast_to(gains[None, None], (2 * dp, 1, 2 * D)),
        ("dp", "ctx"), 0, 0, axis_index_groups=groups,
    )
    gains = jnp.sum(spread, axis=(0, 1))
    dk, dv = call_finish(own, other, key_raw[0], k_gain, prepared[2], prepared[3])
    return (output[None], dq[None], dk[None], dv[None], gains[:D], gains[D:])


def solution(mesh):
    return jax.shard_map(
        body,
        mesh=mesh,
        in_specs=(
            P("dp", "ctx", None),
            P("dp", "ctx", None),
            P("dp", "ctx", None),
            P("dp", "ctx", None),
            P("dp", None),
            P(),
            P(),
        ),
        out_specs=(
            P("dp", "ctx", None),
            P("dp", "ctx", None),
            P("dp", "ctx", None),
            P("dp", "ctx", None),
            P(),
            P(),
        ),
        check_vma=False,
    )
```

```python
import functools
import math

import jax
import jax.numpy as jnp
from jax import lax
from jax.experimental import pallas as pl
from jax.experimental.pallas import tpu as pltpu
from jax.sharding import PartitionSpec as P

rope_theta = 1000000.0
norm_epsilon = 1e-06
masked_value = -1e30
D = 128
F32 = jnp.float32
BF16 = jnp.bfloat16
VM = pl.BlockSpec(memory_space=pltpu.VMEM)
SM = pl.BlockSpec(memory_space=pltpu.SMEM)
SCALE = D ** (-0.5)
LOG2E = math.log2(math.e)


def dot(a, b):
    return jnp.dot(a, b, preferred_element_type=F32)


def sin_cos(angle):
    turns = jnp.floor(angle * (2.0 / math.pi) + 0.5)
    r = angle - turns * 1.5703125
    r = r - turns * 4.837512969970703125e-4
    r = r - turns * 7.549789948768648e-8
    r2 = r * r
    s = r + r * r2 * (-1.6666654611e-1 + r2 * (8.3321608736e-3 + r2 * -1.9515295891e-4))
    c = 1.0 - 0.5 * r2 + r2 * r2 * (
        4.166664568298827e-2 + r2 * (-1.388731625493765e-3 + r2 * 2.443315711809948e-5)
    )
    quarter = turns.astype(jnp.int32)
    odd = (quarter & 1) == 1
    sin_part = jnp.where(odd, c, s)
    cos_part = jnp.where(odd, s, c)
    sin_part = jnp.where((quarter & 2) == 2, -sin_part, sin_part)
    cos_part = jnp.where(((quarter + 1) & 2) == 2, -cos_part, cos_part)
    return sin_part, cos_part


def starts_of(lengths, tokens):
    end = jnp.int32(0)
    start = jnp.zeros_like(tokens)
    for d in range(lengths.shape[1]):
        end = end + lengths[0, d]
        start = jnp.where(tokens >= end, end, start)
    return start


def unfold(table):
    turned = pltpu.roll(table, D // 2, 1)
    first_lanes = lax.broadcasted_iota(jnp.int32, table.shape, 1) < D // 2
    return jnp.where(first_lanes, table, turned), jnp.where(first_lanes, -turned, table)


def rotate(x, cosine, sine):
    return x * cosine + pltpu.roll(x, D // 2, 1) * sine


def rotate_back(x, cosine, sine):
    return x * cosine - pltpu.roll(x, D // 2, 1) * sine


def unit_of(raw):
    x = raw.astype(F32)
    inverse = lax.rsqrt(jnp.mean(x * x, axis=1, keepdims=True) + norm_epsilon)
    return x * inverse, inverse


def prep_kernel(
    heads, token_ref, lengths, freq, q_raw, dout, gain_ref,
    table_ref, table_own, q_ref, qt_ref, do_ref, dot_ref, pos_ref,
):
    tokens_own = q_raw.shape[0]
    seq = table_ref.shape[0]
    row = lax.broadcasted_iota(jnp.int32, (D, D), 0)
    lane = lax.broadcasted_iota(jnp.int32, (D, D), 1)
    tokens = row * D + lane
    positions = tokens - starts_of(lengths, tokens)
    pos_ref[...] = positions.astype(F32).T
    first_lanes = lane < D // 2
    for i in range(seq // D):
        angle = pos_ref[:, i : i + 1] * freq[...]
        s, c = sin_cos(angle)
        table_ref[i * D : (i + 1) * D, :] = jnp.where(first_lanes, c, s)
    first = pl.multiple_of(token_ref[0], tokens_own)
    mine = table_ref[pl.ds(first, tokens_own), :]
    table_own[...] = mine
    cosine, sine = unfold(mine)
    for h in range(heads):
        cols = slice(h * D, (h + 1) * D)
        rows = slice(h * tokens_own, (h + 1) * tokens_own)
        unit, _ = unit_of(q_raw[:, cols])
        q = rotate(unit * gain_ref[0:1, :], cosine, sine)
        q_ref[rows, :] = q.astype(BF16)
        qt_ref[:, rows] = q.T.astype(BF16)
        g = dout[:, cols]
        do_ref[rows, :] = g
        dot_ref[:, rows] = g.astype(F32).T.astype(BF16)


def attend_kernel(
    heads, token_ref, lengths, kv_own, kv_other, table_ref, table_own, q_ref, qt_ref, do_ref, dot_ref,
    q_raw, gain_ref,
    out_ref, dq_ref, dkv_ref, gains_ref,
    s_buf, k_buf, kt_buf, vt_buf, ot_buf, dqt_buf, max_buf, sum_buf, row_buf, kg_buf,
):
    blocks, tokens_own, _ = kv_own.shape
    kb = 2 * tokens_own
    cols_all = heads * tokens_own
    cc = 2 * tokens_own
    chunks = cols_all // cc
    first = token_ref[0]
    end = jnp.int32(0)
    low = jnp.int32(0)
    for d in range(lengths.shape[1]):
        end = end + lengths[0, d]
        low = jnp.where(end <= first, end, low)
    lo = low // kb
    hi = (first + tokens_own - 1) // kb + 1
    tok = first + lax.broadcasted_iota(jnp.int32, (8, tokens_own), 1)
    start_row = starts_of(lengths, tok)[:1]
    tok_row = tok[:1]
    dkv_ref[...] = jnp.zeros_like(dkv_ref)
    max_buf[...] = jnp.full_like(max_buf, masked_value)
    sum_buf[...] = jnp.zeros_like(sum_buf)
    ot_buf[...] = jnp.zeros_like(ot_buf)
    dqt_buf[...] = jnp.zeros_like(dqt_buf)
    kg_buf[...] = jnp.zeros_like(kg_buf)
    factor = SCALE * LOG2E

    side = (first // tokens_own) % 2

    def tables(b):
        start = b * kb
        own = pl.multiple_of(start + side * tokens_own, tokens_own)
        other = pl.multiple_of(start + (1 - side) * tokens_own, tokens_own)
        rows = [table_ref[pl.ds(own, tokens_own), :], table_ref[pl.ds(other, tokens_own), :]]
        return unfold(jnp.concatenate(rows, 0))

    def keys_of(b):
        return jnp.concatenate([kv_own[b, :, :D], kv_other[b, :, :D]], 0)

    def values_of(b):
        return jnp.concatenate([kv_own[b, :, D:], kv_other[b, :, D:]], 0)

    row = lax.broadcasted_iota(jnp.int32, (kb, tokens_own), 0)
    key_shift = row + jnp.where(row < tokens_own, side * tokens_own, -side * tokens_own)

    def scores_step(b, carry):
        unit, _ = unit_of(keys_of(b))
        k = rotate(unit * gain_ref[1:2, :], *tables(b))
        k_rows = k.astype(BF16)
        k_buf[b] = k_rows
        kt_buf[b] = k.T.astype(BF16)
        vt_buf[b] = values_of(b).astype(F32).T.astype(BF16)
        key = b * kb + key_shift
        allowed = (key >= start_row) & (key <= tok_row)
        bias = jnp.where(allowed, 0.0, masked_value)
        for c in range(chunks):
            cs = slice(c * cc, (c + 1) * cc)
            s = dot(k_rows, qt_ref[:, cs]) * factor + jnp.concatenate([bias, bias], 1)
            s_buf[b, :, cs] = s
            max_buf[:, cs] = jnp.maximum(max_buf[:, cs], jnp.max(s.reshape(kb // 8, 8, cc), axis=0))
        return carry

    lax.fori_loop(lo, hi, scores_step, 0)
    row_buf[:1, :] = jnp.max(max_buf[...], axis=0, keepdims=True)

    def exp_step(b, carry):
        for c in range(chunks):
            cs = slice(c * cc, (c + 1) * cc)
            e = jnp.exp2(s_buf[b, :, cs] - row_buf[:1, cs])
            s_buf[b, :, cs] = e
            sum_buf[:, cs] += jnp.sum(e.reshape(kb // 8, 8, cc), axis=0)
            ot_buf[:, cs] += dot(vt_buf[b], e.astype(BF16))
        return carry

    lax.fori_loop(lo, hi, exp_step, 0)
    sum_buf[:1, :] = 1.0 / jnp.sum(sum_buf[...], axis=0, keepdims=True)
    for h in range(heads):
        hs = slice(h * tokens_own, (h + 1) * tokens_own)
        ot = (ot_buf[:, hs] * sum_buf[:1, hs]).astype(BF16).astype(F32)
        out_ref[:, h * D : (h + 1) * D] = ot.T.astype(BF16)
        row_buf[:1, hs] = jnp.sum(ot * dot_ref[:, hs].astype(F32), axis=0, keepdims=True)

    def back_step(b, carry):
        dk = jnp.zeros((kb, D), F32)
        dv = jnp.zeros((kb, D), F32)
        v_rows = values_of(b)
        for c in range(chunks):
            cs = slice(c * cc, (c + 1) * cc)
            dp = dot(v_rows, dot_ref[:, cs])
            prob = s_buf[b, :, cs] * sum_buf[:1, cs]
            dv = dv + dot(prob.astype(BF16), do_ref[cs, :])
            ds = (prob * (dp - row_buf[:1, cs])).astype(BF16)
            dk = dk + dot(ds, q_ref[cs, :])
            dqt_buf[:, cs] += dot(kt_buf[b], ds)
        dk = dk * SCALE
        dkv_ref[b, :, :D] = dk.astype(BF16)
        dkv_ref[b, :, D:] = dv.astype(BF16)
        unit, _ = unit_of(keys_of(b))
        terms = rotate_back(dk, *tables(b)) * unit
        kg_buf[...] += jnp.sum(terms.reshape(kb // 8, 8, D), axis=0)
        return carry

    lax.fori_loop(lo, hi, back_step, 0)
    cosine, sine = unfold(table_own[...])
    q_sum = jnp.zeros((8, D), F32)
    for h in range(heads):
        hs = slice(h * tokens_own, (h + 1) * tokens_own)
        back = rotate_back(dqt_buf[:, hs].T * SCALE, cosine, sine)
        unit, inverse = unit_of(q_raw[:, h * D : (h + 1) * D])
        q_sum = q_sum + jnp.sum((back * unit).reshape(tokens_own // 8, 8, D), axis=0)
        scaled = back * gain_ref[0:1, :]
        mean = jnp.mean(scaled * unit, axis=1, keepdims=True)
        dq_ref[:, h * D : (h + 1) * D] = (inverse * (scaled - unit * mean)).astype(BF16)
    gains_ref[:, :D] = jnp.broadcast_to(jnp.sum(q_sum, axis=0, keepdims=True), (8, D))
    gains_ref[:, D:] = jnp.broadcast_to(jnp.sum(kg_buf[...], axis=0, keepdims=True), (8, D))


def finish_kernel(own_ref, other_ref, k_raw, gain_ref, table_own, dk_ref, dv_ref):
    total = own_ref[...] + other_ref[...].astype(F32)
    unit, inverse = unit_of(k_raw[...])
    back = rotate_back(total[:, :D], *unfold(table_own[...]))
    scaled = back * gain_ref[1:2, :]
    mean = jnp.mean(scaled * unit, axis=1, keepdims=True)
    dk_ref[...] = (inverse * (scaled - unit * mean)).astype(BF16)
    dv_ref[...] = total[:, D:].astype(BF16)


def call_prep(token, lengths, freq, q_raw, dout, both_gains, seq, **kw):
    tokens_own, width = q_raw.shape
    heads = width // D
    rows = heads * tokens_own
    shapes = [
        ((seq, D), F32), ((tokens_own, D), F32),
        ((rows, D), BF16), ((D, rows), BF16), ((rows, D), BF16), ((D, rows), BF16),
    ]
    return pl.pallas_call(
        functools.partial(prep_kernel, heads),
        out_shape=[jax.ShapeDtypeStruct(s, t) for s, t in shapes],
        in_specs=[SM, SM, VM, VM, VM, VM],
        out_specs=[VM] * len(shapes),
        scratch_shapes=[pltpu.VMEM((D, D), F32)],
        compiler_params=pltpu.CompilerParams(vmem_limit_bytes=12 * 2**20),
        cost_estimate=pl.CostEstimate(flops=40_000_000, bytes_accessed=4_000_000, transcendentals=0),
        name="prep",
        **kw,
    )(token, lengths, freq, q_raw, dout, both_gains)


def call_attend(token, lengths, kv_own, kv_other, prepared, q_raw, both_gains, **kw):
    tokens_own, width = q_raw.shape
    heads = width // D
    blocks = kv_own.shape[0]
    kb = 2 * tokens_own
    rows = heads * tokens_own
    shapes = [
        ((tokens_own, width), BF16), ((tokens_own, width), BF16), ((blocks, kb, 2 * D), BF16), ((8, 2 * D), F32),
    ]
    scratch = [
        pltpu.VMEM((blocks, kb, rows), F32),
        pltpu.VMEM((blocks, kb, D), BF16), pltpu.VMEM((blocks, D, kb), BF16),
        pltpu.VMEM((blocks, D, kb), BF16), pltpu.VMEM((D, rows), F32), pltpu.VMEM((D, rows), F32),
        pltpu.VMEM((8, rows), F32), pltpu.VMEM((8, rows), F32), pltpu.VMEM((8, rows), F32),
        pltpu.VMEM((8, D), F32),
    ]
    return pl.pallas_call(
        functools.partial(attend_kernel, heads),
        out_shape=[jax.ShapeDtypeStruct(s, t) for s, t in shapes],
        in_specs=[SM, SM] + [VM] * 10,
        out_specs=[VM] * len(shapes),
        scratch_shapes=scratch,
        compiler_params=pltpu.CompilerParams(vmem_limit_bytes=20 * 2**20),
        cost_estimate=pl.CostEstimate(flops=3_200_000_000, bytes_accessed=8_000_000, transcendentals=2_000_000),
        name="attend",
        **kw,
    )(token, lengths, kv_own, kv_other, *prepared, q_raw, both_gains)


def call_finish(own, other, k_raw, both_gains, table_own, **kw):
    shape = jax.ShapeDtypeStruct(k_raw.shape, BF16)
    return pl.pallas_call(
        finish_kernel,
        out_shape=[shape, shape],
        in_specs=[VM] * 5,
        out_specs=[VM] * 2,
        name="finish",
        **kw,
    )(own, other, k_raw, both_gains, table_own)


def frequency_row():
    exponent = jnp.arange(D // 2, dtype=F32) * (2.0 / D)
    frequency = jnp.power(F32(rope_theta), -exponent)
    return jnp.concatenate([frequency, frequency])[None, :]


def strided(size, stride, count):
    span = stride * count
    return [
        [base + low + stride * k for k in range(count)]
        for base in range(0, size, span)
        for low in range(stride)
    ]


def body(query_raw, key_raw, values, out_grad, doc_lengths, query_gain, key_gain):
    tokens_own = query_raw.shape[1]
    ctx = lax.axis_size("ctx")
    dp = lax.axis_size("dp")
    seq = tokens_own * ctx
    half = ctx // 2
    me = lax.axis_index("ctx")
    token = (me * tokens_own)[None].astype(jnp.int32)
    both_gains = jnp.stack([query_gain, key_gain] * 4)
    columns = [[2 * y + z for y in range(half)] for z in range(2)]
    swap = [(i, i ^ 1) for i in range(ctx)]

    def exchange(blocks):
        return lax.all_to_all(blocks, "ctx", 0, 0, axis_index_groups=columns)

    def spread(rows):
        return jnp.broadcast_to(rows[None], (half,) + rows.shape)

    kv = jnp.concatenate([key_raw[0], values[0]], axis=1)
    kv_swapped = lax.ppermute(kv, "ctx", swap)
    kv_own = exchange(spread(kv))
    kv_other = exchange(spread(kv_swapped))
    prepared = call_prep(token, doc_lengths, frequency_row(), query_raw[0], out_grad[0], both_gains, seq)
    output, dq, parts, gains = call_attend(
        token, doc_lengths, kv_own, kv_other, prepared, query_raw[0], both_gains
    )
    received = exchange(parts)
    own = jnp.sum(received[:, :tokens_own].astype(F32), axis=0)
    theirs = jnp.sum(received[:, tokens_own:].astype(F32), axis=0).astype(BF16)
    gains = lax.psum(gains[0], "dp", axis_index_groups=strided(dp, 1, 2))
    gains = lax.psum(gains, "dp", axis_index_groups=strided(dp, 8, dp // 8))
    gains = lax.psum(gains, "ctx", axis_index_groups=strided(ctx, 1, 2))
    other = lax.ppermute(theirs, "ctx", swap)
    own, gains = lax.optimization_barrier((own, gains))
    groups = [
        [(8 * x + 2 * z + core) * ctx + 2 * y + side for z in range(4) for y in range(half)]
        for x in range(dp // 8) for core in range(2) for side in range(2)
    ]
    gains = lax.all_to_all(
        jnp.broadcast_to(gains[None, None], (4 * half, 1, 2 * D)), ("dp", "ctx"), 0, 0, axis_index_groups=groups
    )
    gains = jnp.sum(gains, axis=(0, 1))
    dk, dv = call_finish(own, other, key_raw[0], both_gains, prepared[1])
    return (output[None], dq[None], dk[None], dv[None], gains[:D], gains[D:])


def solution(mesh):
    return jax.shard_map(
        body,
        mesh=mesh,
        in_specs=(
            P("dp", "ctx", None),
            P("dp", "ctx", None),
            P("dp", "ctx", None),
            P("dp", "ctx", None),
            P("dp", None),
            P(),
            P(),
        ),
        out_specs=(
            P("dp", "ctx", None),
            P("dp", "ctx", None),
            P("dp", "ctx", None),
            P("dp", "ctx", None),
            P(),
            P(),
        ),
        check_vma=False,
    )
```

```python
import functools
import math

import jax
import jax.numpy as jnp
from jax import lax
from jax.experimental import pallas as pl
from jax.experimental.pallas import tpu as pltpu
from jax.sharding import PartitionSpec as P

rope_theta = 1000000.0
norm_epsilon = 1e-06
masked_value = -1e30
D = 128
F32 = jnp.float32
BF16 = jnp.bfloat16
VM = pl.BlockSpec(memory_space=pltpu.VMEM)
SM = pl.BlockSpec(memory_space=pltpu.SMEM)
SCALE = D ** (-0.5)
LOG2E = math.log2(math.e)


def dot(a, b):
    return jnp.dot(a, b, preferred_element_type=F32)


def sin_cos(angle):
    turns = jnp.floor(angle * (2.0 / math.pi) + 0.5)
    r = angle - turns * 1.5703125
    r = r - turns * 4.837512969970703125e-4
    r = r - turns * 7.549789948768648e-8
    r2 = r * r
    s = r + r * r2 * (-1.6666654611e-1 + r2 * (8.3321608736e-3 + r2 * -1.9515295891e-4))
    c = 1.0 - 0.5 * r2 + r2 * r2 * (
        4.166664568298827e-2 + r2 * (-1.388731625493765e-3 + r2 * 2.443315711809948e-5)
    )
    quarter = turns.astype(jnp.int32)
    odd = (quarter & 1) == 1
    sin_part = jnp.where(odd, c, s)
    cos_part = jnp.where(odd, s, c)
    sin_part = jnp.where((quarter & 2) == 2, -sin_part, sin_part)
    cos_part = jnp.where(((quarter + 1) & 2) == 2, -cos_part, cos_part)
    return sin_part, cos_part


def starts_of(lengths, tokens):
    end = jnp.int32(0)
    start = jnp.zeros_like(tokens)
    for d in range(lengths.shape[1]):
        end = end + lengths[0, d]
        start = jnp.where(tokens >= end, end, start)
    return start


def unfold(table):
    turned = pltpu.roll(table, D // 2, 1)
    first_lanes = lax.broadcasted_iota(jnp.int32, table.shape, 1) < D // 2
    return jnp.where(first_lanes, table, turned), jnp.where(first_lanes, -turned, table)


def rotate(x, cosine, sine):
    return x * cosine + pltpu.roll(x, D // 2, 1) * sine


def rotate_back(x, cosine, sine):
    return x * cosine - pltpu.roll(x, D // 2, 1) * sine


def unit_of(raw):
    x = raw.astype(F32)
    inverse = lax.rsqrt(jnp.mean(x * x, axis=1, keepdims=True) + norm_epsilon)
    return x * inverse, inverse


def prep_kernel(
    heads, token_ref, lengths, freq, q_raw, dout, gain_ref,
    table_ref, table_own, q_ref, qt_ref, do_ref, dot_ref, pos_ref,
):
    tokens_own = q_raw.shape[0]
    seq = table_ref.shape[0]
    row = lax.broadcasted_iota(jnp.int32, (D, D), 0)
    lane = lax.broadcasted_iota(jnp.int32, (D, D), 1)
    tokens = row * D + lane
    positions = tokens - starts_of(lengths, tokens)
    pos_ref[...] = positions.astype(F32).T
    first_lanes = lane < D // 2
    for i in range(seq // D):
        angle = pos_ref[:, i : i + 1] * freq[...]
        s, c = sin_cos(angle)
        table_ref[i * D : (i + 1) * D, :] = jnp.where(first_lanes, c, s)
    first = pl.multiple_of(token_ref[0], tokens_own)
    mine = table_ref[pl.ds(first, tokens_own), :]
    table_own[...] = mine
    cosine, sine = unfold(mine)
    for h in range(heads):
        cols = slice(h * D, (h + 1) * D)
        rows = slice(h * tokens_own, (h + 1) * tokens_own)
        unit, _ = unit_of(q_raw[:, cols])
        q = rotate(unit * gain_ref[0:1, :], cosine, sine)
        q_ref[rows, :] = q.astype(BF16)
        qt_ref[:, rows] = q.T.astype(BF16)
        g = dout[:, cols]
        do_ref[rows, :] = g
        dot_ref[:, rows] = g.astype(F32).T.astype(BF16)


def attend_kernel(
    heads, token_ref, lengths, kv_own, kv_other, table_ref, table_own, q_ref, qt_ref, do_ref, dot_ref,
    q_raw, gain_ref,
    out_ref, dq_ref, dkv_ref, gains_ref,
    s_buf, k_buf, kt_buf, vt_buf, ot_buf, dqt_buf, max_buf, sum_buf, row_buf, kg_buf,
):
    _, tokens_own, _ = kv_own.shape
    kb = 4 * tokens_own
    blocks = kv_own.shape[0] // 2
    cols_all = heads * tokens_own
    cc = cols_all
    chunks = cols_all // cc
    first = token_ref[0]
    end = jnp.int32(0)
    low = jnp.int32(0)
    for d in range(lengths.shape[1]):
        end = end + lengths[0, d]
        low = jnp.where(end <= first, end, low)
    lo = low // kb
    hi = (first + tokens_own - 1) // kb + 1
    tok = first + lax.broadcasted_iota(jnp.int32, (8, tokens_own), 1)
    start_row = starts_of(lengths, tok)[:1]
    tok_row = tok[:1]
    dkv_ref[...] = jnp.zeros_like(dkv_ref)
    max_buf[...] = jnp.full_like(max_buf, masked_value)
    sum_buf[...] = jnp.zeros_like(sum_buf)
    ot_buf[...] = jnp.zeros_like(ot_buf)
    dqt_buf[...] = jnp.zeros_like(dqt_buf)
    kg_buf[...] = jnp.zeros_like(kg_buf)
    factor = SCALE * LOG2E

    side = (first // tokens_own) % 2

    def tables(b):
        rows = []
        for i in range(2):
            for s in (side, 1 - side):
                start = b * kb + (2 * i + s) * tokens_own
                rows.append(table_ref[pl.ds(pl.multiple_of(start, tokens_own), tokens_own), :])
        return unfold(jnp.concatenate(rows, 0))

    def keys_of(b):
        return jnp.concatenate([kv_own[2 * b, :, :D], kv_other[2 * b, :, :D], kv_own[2 * b + 1, :, :D], kv_other[2 * b + 1, :, :D]], 0)

    def values_of(b):
        return jnp.concatenate([kv_own[2 * b, :, D:], kv_other[2 * b, :, D:], kv_own[2 * b + 1, :, D:], kv_other[2 * b + 1, :, D:]], 0)

    row = lax.broadcasted_iota(jnp.int32, (kb, tokens_own), 0)
    key_shift = row + jnp.where(row % (2 * tokens_own) < tokens_own, side * tokens_own, -side * tokens_own)

    def scores_step(b, carry):
        unit, _ = unit_of(keys_of(b))
        k = rotate(unit * gain_ref[1:2, :], *tables(b))
        k_rows = k.astype(BF16)
        k_buf[b] = k_rows
        kt_buf[b] = k.T.astype(BF16)
        vt_buf[b] = values_of(b).astype(F32).T.astype(BF16)
        key = b * kb + key_shift
        allowed = (key >= start_row) & (key <= tok_row)
        bias = jnp.where(allowed, 0.0, masked_value)
        for c in range(chunks):
            cs = slice(c * cc, (c + 1) * cc)
            s = dot(k_rows, qt_ref[:, cs]) * factor + jnp.concatenate([bias] * (cc // tokens_own), 1)
            s_buf[b, :, cs] = s
            max_buf[:, cs] = jnp.maximum(max_buf[:, cs], jnp.max(s.reshape(kb // 8, 8, cc), axis=0))
        return carry

    lax.fori_loop(lo, hi, scores_step, 0)
    row_buf[:1, :] = jnp.max(max_buf[...], axis=0, keepdims=True)

    def exp_step(b, carry):
        for c in range(chunks):
            cs = slice(c * cc, (c + 1) * cc)
            e = jnp.exp2(s_buf[b, :, cs] - row_buf[:1, cs])
            s_buf[b, :, cs] = e
            sum_buf[:, cs] += jnp.sum(e.reshape(kb // 8, 8, cc), axis=0)
            ot_buf[:, cs] += dot(vt_buf[b], e.astype(BF16))
        return carry

    lax.fori_loop(lo, hi, exp_step, 0)
    sum_buf[:1, :] = 1.0 / jnp.sum(sum_buf[...], axis=0, keepdims=True)
    for h in range(heads):
        hs = slice(h * tokens_own, (h + 1) * tokens_own)
        ot = (ot_buf[:, hs] * sum_buf[:1, hs]).astype(BF16).astype(F32)
        out_ref[:, h * D : (h + 1) * D] = ot.T.astype(BF16)
        row_buf[:1, hs] = jnp.sum(ot * dot_ref[:, hs].astype(F32), axis=0, keepdims=True)

    def back_step(b, carry):
        dk = jnp.zeros((kb, D), F32)
        dv = jnp.zeros((kb, D), F32)
        v_rows = values_of(b)
        for c in range(chunks):
            cs = slice(c * cc, (c + 1) * cc)
            dp = dot(v_rows, dot_ref[:, cs])
            prob = s_buf[b, :, cs] * sum_buf[:1, cs]
            dv = dv + dot(prob.astype(BF16), do_ref[cs, :])
            ds = (prob * (dp - row_buf[:1, cs])).astype(BF16)
            dk = dk + dot(ds, q_ref[cs, :])
            dqt_buf[:, cs] += dot(kt_buf[b], ds)
        dk = dk * SCALE
        for i in range(2):
            half = slice(i * 2 * tokens_own, (i + 1) * 2 * tokens_own)
            dkv_ref[2 * b + i, :, :D] = dk[half].astype(BF16)
            dkv_ref[2 * b + i, :, D:] = dv[half].astype(BF16)
        unit, _ = unit_of(keys_of(b))
        terms = rotate_back(dk, *tables(b)) * unit
        kg_buf[...] += jnp.sum(terms.reshape(kb // 8, 8, D), axis=0)
        return carry

    lax.fori_loop(lo, hi, back_step, 0)
    cosine, sine = unfold(table_own[...])
    q_sum = jnp.zeros((8, D), F32)
    for h in range(heads):
        hs = slice(h * tokens_own, (h + 1) * tokens_own)
        back = rotate_back(dqt_buf[:, hs].T * SCALE, cosine, sine)
        unit, inverse = unit_of(q_raw[:, h * D : (h + 1) * D])
        q_sum = q_sum + jnp.sum((back * unit).reshape(tokens_own // 8, 8, D), axis=0)
        scaled = back * gain_ref[0:1, :]
        mean = jnp.mean(scaled * unit, axis=1, keepdims=True)
        dq_ref[:, h * D : (h + 1) * D] = (inverse * (scaled - unit * mean)).astype(BF16)
    gains_ref[:, :D] = jnp.broadcast_to(jnp.sum(q_sum, axis=0, keepdims=True), (8, D))
    gains_ref[:, D:] = jnp.broadcast_to(jnp.sum(kg_buf[...], axis=0, keepdims=True), (8, D))


def finish_kernel(own_ref, other_ref, k_raw, gain_ref, table_own, dk_ref, dv_ref):
    total = own_ref[...] + other_ref[...].astype(F32)
    unit, inverse = unit_of(k_raw[...])
    back = rotate_back(total[:, :D], *unfold(table_own[...]))
    scaled = back * gain_ref[1:2, :]
    mean = jnp.mean(scaled * unit, axis=1, keepdims=True)
    dk_ref[...] = (inverse * (scaled - unit * mean)).astype(BF16)
    dv_ref[...] = total[:, D:].astype(BF16)


def call_prep(token, lengths, freq, q_raw, dout, both_gains, seq, **kw):
    tokens_own, width = q_raw.shape
    heads = width // D
    rows = heads * tokens_own
    shapes = [
        ((seq, D), F32), ((tokens_own, D), F32),
        ((rows, D), BF16), ((D, rows), BF16), ((rows, D), BF16), ((D, rows), BF16),
    ]
    return pl.pallas_call(
        functools.partial(prep_kernel, heads),
        out_shape=[jax.ShapeDtypeStruct(s, t) for s, t in shapes],
        in_specs=[SM, SM, VM, VM, VM, VM],
        out_specs=[VM] * len(shapes),
        scratch_shapes=[pltpu.VMEM((D, D), F32)],
        compiler_params=pltpu.CompilerParams(vmem_limit_bytes=12 * 2**20),
        cost_estimate=pl.CostEstimate(flops=40_000_000, bytes_accessed=4_000_000, transcendentals=0),
        name="prep",
        **kw,
    )(token, lengths, freq, q_raw, dout, both_gains)


def call_attend(token, lengths, kv_own, kv_other, prepared, q_raw, both_gains, **kw):
    tokens_own, width = q_raw.shape
    heads = width // D
    blocks = kv_own.shape[0] // 2
    kb = 4 * tokens_own
    rows = heads * tokens_own
    shapes = [
        ((tokens_own, width), BF16), ((tokens_own, width), BF16), ((2 * blocks, kb // 2, 2 * D), BF16), ((8, 2 * D), F32),
    ]
    scratch = [
        pltpu.VMEM((blocks, kb, rows), F32),
        pltpu.VMEM((blocks, kb, D), BF16), pltpu.VMEM((blocks, D, kb), BF16),
        pltpu.VMEM((blocks, D, kb), BF16), pltpu.VMEM((D, rows), F32), pltpu.VMEM((D, rows), F32),
        pltpu.VMEM((8, rows), F32), pltpu.VMEM((8, rows), F32), pltpu.VMEM((8, rows), F32),
        pltpu.VMEM((8, D), F32),
    ]
    return pl.pallas_call(
        functools.partial(attend_kernel, heads),
        out_shape=[jax.ShapeDtypeStruct(s, t) for s, t in shapes],
        in_specs=[SM, SM] + [VM] * 10,
        out_specs=[VM] * len(shapes),
        scratch_shapes=scratch,
        compiler_params=pltpu.CompilerParams(vmem_limit_bytes=20 * 2**20),
        cost_estimate=pl.CostEstimate(flops=3_200_000_000, bytes_accessed=8_000_000, transcendentals=2_000_000),
        name="attend",
        **kw,
    )(token, lengths, kv_own, kv_other, *prepared, q_raw, both_gains)


def call_finish(own, other, k_raw, both_gains, table_own, **kw):
    shape = jax.ShapeDtypeStruct(k_raw.shape, BF16)
    return pl.pallas_call(
        finish_kernel,
        out_shape=[shape, shape],
        in_specs=[VM] * 5,
        out_specs=[VM] * 2,
        cost_estimate=pl.CostEstimate(flops=0, bytes_accessed=100_000_000, transcendentals=0),
        name="finish",
        **kw,
    )(own, other, k_raw, both_gains, table_own)


def frequency_row():
    exponent = jnp.arange(D // 2, dtype=F32) * (2.0 / D)
    frequency = jnp.power(F32(rope_theta), -exponent)
    return jnp.concatenate([frequency, frequency])[None, :]


def strided(size, stride, count):
    span = stride * count
    return [
        [base + low + stride * k for k in range(count)]
        for base in range(0, size, span)
        for low in range(stride)
    ]


def body(query_raw, key_raw, values, out_grad, doc_lengths, query_gain, key_gain):
    tokens_own = query_raw.shape[1]
    ctx = lax.axis_size("ctx")
    dp = lax.axis_size("dp")
    seq = tokens_own * ctx
    half = ctx // 2
    me = lax.axis_index("ctx")
    token = (me * tokens_own)[None].astype(jnp.int32)
    both_gains = jnp.stack([query_gain, key_gain] * 4)
    columns = [[2 * y + z for y in range(half)] for z in range(2)]
    swap = [(i, i ^ 1) for i in range(ctx)]

    def exchange(blocks):
        return lax.all_to_all(blocks, "ctx", 0, 0, axis_index_groups=columns)

    def spread(rows):
        return jnp.broadcast_to(rows[None], (half,) + rows.shape)

    kv = jnp.concatenate([key_raw[0], values[0]], axis=1)
    kv_swapped = lax.ppermute(kv, "ctx", swap)
    kv_own = exchange(spread(kv))
    kv_other = exchange(spread(kv_swapped))
    prepared = call_prep(token, doc_lengths, frequency_row(), query_raw[0], out_grad[0], both_gains, seq)
    output, dq, parts, gains = call_attend(
        token, doc_lengths, kv_own, kv_other, prepared, query_raw[0], both_gains
    )
    received = exchange(parts)
    own = jnp.sum(received[:, :tokens_own].astype(F32), axis=0)
    theirs = jnp.sum(received[:, tokens_own:].astype(F32), axis=0).astype(BF16)
    gains = lax.psum(gains[0], "dp", axis_index_groups=strided(dp, 1, 2))
    gains = lax.psum(gains, "dp", axis_index_groups=strided(dp, 8, dp // 8))
    gains = lax.psum(gains, "ctx", axis_index_groups=strided(ctx, 1, 2))
    other = lax.ppermute(theirs, "ctx", swap)
    own, gains = lax.optimization_barrier((own, gains))
    groups = [
        [(8 * x + 2 * z + core) * ctx + 2 * y + side for z in range(4) for y in range(half)]
        for x in range(dp // 8) for core in range(2) for side in range(2)
    ]
    gains = lax.all_to_all(
        jnp.broadcast_to(gains[None, None], (4 * half, 1, 2 * D)), ("dp", "ctx"), 0, 0, axis_index_groups=groups
    )
    gains = jnp.sum(gains, axis=(0, 1))
    dk, dv = call_finish(own, other, key_raw[0], both_gains, prepared[1])
    return (output[None], dq[None], dk[None], dv[None], gains[:D], gains[D:])


def solution(mesh):
    return jax.shard_map(
        body,
        mesh=mesh,
        in_specs=(
            P("dp", "ctx", None),
            P("dp", "ctx", None),
            P("dp", "ctx", None),
            P("dp", "ctx", None),
            P("dp", None),
            P(),
            P(),
        ),
        out_specs=(
            P("dp", "ctx", None),
            P("dp", "ctx", None),
            P("dp", "ctx", None),
            P("dp", "ctx", None),
            P(),
            P(),
        ),
        check_vma=False,
    )
```

```python
import functools
import math

import jax
import jax.numpy as jnp
from jax import lax
from jax.experimental import pallas as pl
from jax.experimental.pallas import tpu as pltpu
from jax.sharding import PartitionSpec as P

rope_theta = 1000000.0
norm_epsilon = 1e-06
masked_value = -1e30
D = 128
F32 = jnp.float32
BF16 = jnp.bfloat16
VM = pl.BlockSpec(memory_space=pltpu.VMEM)
SM = pl.BlockSpec(memory_space=pltpu.SMEM)
SCALE = D ** (-0.5)
LOG2E = math.log2(math.e)


def dot(a, b):
    return jnp.dot(a, b, preferred_element_type=F32)


def dot_rows(a, b):
    return lax.dot_general(a, b, (((1,), (1,)), ((), ())), preferred_element_type=F32)


def sin_cos(angle):
    turns = jnp.floor(angle * (2.0 / math.pi) + 0.5)
    r = angle - turns * 1.5703125
    r = r - turns * 4.837512969970703125e-4
    r = r - turns * 7.549789948768648e-8
    r2 = r * r
    s = r + r * r2 * (-1.6666654611e-1 + r2 * (8.3321608736e-3 + r2 * -1.9515295891e-4))
    c = 1.0 - 0.5 * r2 + r2 * r2 * (
        4.166664568298827e-2 + r2 * (-1.388731625493765e-3 + r2 * 2.443315711809948e-5)
    )
    quarter = turns.astype(jnp.int32)
    odd = (quarter & 1) == 1
    sin_part = jnp.where(odd, c, s)
    cos_part = jnp.where(odd, s, c)
    sin_part = jnp.where((quarter & 2) == 2, -sin_part, sin_part)
    cos_part = jnp.where(((quarter + 1) & 2) == 2, -cos_part, cos_part)
    return sin_part, cos_part


def starts_of(lengths, tokens):
    end = jnp.int32(0)
    start = jnp.zeros_like(tokens)
    for d in range(lengths.shape[1]):
        end = end + lengths[0, d]
        start = jnp.where(tokens >= end, end, start)
    return start


def unfold(table):
    turned = pltpu.roll(table, D // 2, 1)
    first_lanes = lax.broadcasted_iota(jnp.int32, table.shape, 1) < D // 2
    return jnp.where(first_lanes, table, turned), jnp.where(first_lanes, -turned, table)


def rotate(x, cosine, sine):
    return x * cosine + pltpu.roll(x, D // 2, 1) * sine


def rotate_back(x, cosine, sine):
    return x * cosine - pltpu.roll(x, D // 2, 1) * sine


def unit_of(raw):
    x = raw.astype(F32)
    inverse = lax.rsqrt(jnp.mean(x * x, axis=1, keepdims=True) + norm_epsilon)
    return x * inverse, inverse


def prep_kernel(
    heads, token_ref, lengths, freq, q_raw, dout, gain_ref,
    table_ref, table_own, q_ref, do_ref, pos_ref,
):
    tokens_own = q_raw.shape[0]
    seq = table_ref.shape[0]
    row = lax.broadcasted_iota(jnp.int32, (D, D), 0)
    lane = lax.broadcasted_iota(jnp.int32, (D, D), 1)
    tokens = row * D + lane
    positions = tokens - starts_of(lengths, tokens)
    pos_ref[...] = positions.astype(F32).T
    first_lanes = lane < D // 2
    for i in range(seq // D):
        angle = pos_ref[:, i : i + 1] * freq[...]
        s, c = sin_cos(angle)
        table_ref[i * D : (i + 1) * D, :] = jnp.where(first_lanes, c, s)
    first = pl.multiple_of(token_ref[0], tokens_own)
    mine = table_ref[pl.ds(first, tokens_own), :]
    table_own[...] = mine
    cosine, sine = unfold(mine)
    for h in range(heads):
        cols = slice(h * D, (h + 1) * D)
        rows = slice(h * tokens_own, (h + 1) * tokens_own)
        unit, _ = unit_of(q_raw[:, cols])
        q = rotate(unit * gain_ref[0:1, :], cosine, sine)
        q_ref[rows, :] = q.astype(BF16)
        do_ref[rows, :] = dout[:, cols]


def attend_kernel(
    heads, token_ref, lengths, kv_own, kv_other, table_ref, q_ref, do_ref, gain_ref,
    out_ref, dqt_buf, dkv_ref, key_sum_ref,
    s_buf, k_buf, kt_buf, vt_buf, ot_buf, max_buf, sum_buf, row_buf, kg_buf,
):
    _, tokens_own, _ = kv_own.shape
    kb = 4 * tokens_own
    blocks = kv_own.shape[0] // 2
    cols_all = heads * tokens_own
    cc = cols_all
    chunks = cols_all // cc
    first = token_ref[0]
    end = jnp.int32(0)
    low = jnp.int32(0)
    for d in range(lengths.shape[1]):
        end = end + lengths[0, d]
        low = jnp.where(end <= first, end, low)
    lo = low // kb
    hi = (first + tokens_own - 1) // kb + 1
    tok = first + lax.broadcasted_iota(jnp.int32, (8, tokens_own), 1)
    start_row = starts_of(lengths, tok)[:1]
    tok_row = tok[:1]
    dkv_ref[...] = jnp.zeros_like(dkv_ref)
    max_buf[...] = jnp.full_like(max_buf, masked_value)
    sum_buf[...] = jnp.zeros_like(sum_buf)
    ot_buf[...] = jnp.zeros_like(ot_buf)
    dqt_buf[...] = jnp.zeros_like(dqt_buf)
    kg_buf[...] = jnp.zeros_like(kg_buf)
    factor = SCALE * LOG2E

    side = (first // tokens_own) % 2

    def tables(b):
        rows = []
        for i in range(2):
            for s in (side, 1 - side):
                start = b * kb + (2 * i + s) * tokens_own
                rows.append(table_ref[pl.ds(pl.multiple_of(start, tokens_own), tokens_own), :])
        return unfold(jnp.concatenate(rows, 0))

    def keys_of(b):
        return jnp.concatenate([kv_own[2 * b, :, :D], kv_other[2 * b, :, :D], kv_own[2 * b + 1, :, :D], kv_other[2 * b + 1, :, :D]], 0)

    def values_of(b):
        return jnp.concatenate([kv_own[2 * b, :, D:], kv_other[2 * b, :, D:], kv_own[2 * b + 1, :, D:], kv_other[2 * b + 1, :, D:]], 0)

    row = lax.broadcasted_iota(jnp.int32, (kb, tokens_own), 0)
    key_shift = row + jnp.where(row % (2 * tokens_own) < tokens_own, side * tokens_own, -side * tokens_own)

    def prepare(b):
        unit, _ = unit_of(keys_of(b))
        k = rotate(unit * gain_ref[1:2, :], *tables(b))
        k_buf[b] = k.astype(BF16)
        kt_buf[b] = k.T.astype(BF16)
        vt_buf[b] = values_of(b).astype(F32).T.astype(BF16)

    def scores_step(b, carry):
        key = b * kb + key_shift
        allowed = (key >= start_row) & (key <= tok_row)
        bias = jnp.where(allowed, 0.0, masked_value)
        for c in range(chunks):
            cs = slice(c * cc, (c + 1) * cc)
            s = dot_rows(k_buf[b], q_ref[cs, :]) * factor + jnp.concatenate([bias] * (cc // tokens_own), 1)
            s_buf[b, :, cs] = s
            max_buf[:, cs] = jnp.maximum(max_buf[:, cs], jnp.max(s.reshape(kb // 8, 8, cc), axis=0))
        prepare(jnp.minimum(b + 1, blocks - 1))
        return carry

    prepare(lo)
    lax.fori_loop(lo, hi, scores_step, 0)
    row_buf[:1, :] = jnp.max(max_buf[...], axis=0, keepdims=True)

    def exp_step(b, carry):
        for c in range(chunks):
            cs = slice(c * cc, (c + 1) * cc)
            e = jnp.exp2(s_buf[b, :, cs] - row_buf[:1, cs])
            s_buf[b, :, cs] = e
            sum_buf[:, cs] += jnp.sum(e.reshape(kb // 8, 8, cc), axis=0)
            ot_buf[:, cs] += dot(vt_buf[b], e.astype(BF16))
        return carry

    lax.fori_loop(lo, hi, exp_step, 0)
    sum_buf[:1, :] = 1.0 / jnp.sum(sum_buf[...], axis=0, keepdims=True)
    for h in range(heads):
        hs = slice(h * tokens_own, (h + 1) * tokens_own)
        ot = (ot_buf[:, hs] * sum_buf[:1, hs]).astype(BF16).astype(F32)
        out_ref[:, h * D : (h + 1) * D] = ot.T.astype(BF16)
        row_buf[:1, hs] = jnp.sum(ot * do_ref[hs, :].T.astype(F32), axis=0, keepdims=True)

    def back_step(b, carry):
        dk = jnp.zeros((kb, D), F32)
        dv = jnp.zeros((kb, D), F32)
        v_rows = values_of(b)
        for c in range(chunks):
            cs = slice(c * cc, (c + 1) * cc)
            dp = dot_rows(v_rows, do_ref[cs, :])
            prob = s_buf[b, :, cs] * sum_buf[:1, cs]
            dv = dv + dot(prob.astype(BF16), do_ref[cs, :])
            ds = (prob * (dp - row_buf[:1, cs])).astype(BF16)
            dk = dk + dot(ds, q_ref[cs, :])
            dqt_buf[:, cs] += dot(kt_buf[b], ds)
        dk = dk * SCALE
        for i in range(2):
            half = slice(i * 2 * tokens_own, (i + 1) * 2 * tokens_own)
            dkv_ref[2 * b + i, :, :D] = dk[half].astype(BF16)
            dkv_ref[2 * b + i, :, D:] = dv[half].astype(BF16)
        unit, _ = unit_of(keys_of(b))
        terms = rotate_back(dk, *tables(b)) * unit
        kg_buf[...] += jnp.sum(terms.reshape(kb // 8, 8, D), axis=0)
        return carry

    lax.fori_loop(lo, hi, back_step, 0)
    key_sum_ref[...] = kg_buf[...]


def query_kernel(heads, dqt_ref, key_sum_ref, table_own, q_raw, gain_ref, dq_ref, gains_ref):
    tokens_own = q_raw.shape[0]
    cosine, sine = unfold(table_own[...])
    q_sum = jnp.zeros((8, D), F32)
    for h in range(heads):
        hs = slice(h * tokens_own, (h + 1) * tokens_own)
        back = rotate_back(dqt_ref[:, hs].T * SCALE, cosine, sine)
        unit, inverse = unit_of(q_raw[:, h * D : (h + 1) * D])
        q_sum = q_sum + jnp.sum((back * unit).reshape(tokens_own // 8, 8, D), axis=0)
        scaled = back * gain_ref[0:1, :]
        mean = jnp.mean(scaled * unit, axis=1, keepdims=True)
        dq_ref[:, h * D : (h + 1) * D] = (inverse * (scaled - unit * mean)).astype(BF16)
    gains_ref[:, :D] = jnp.broadcast_to(jnp.sum(q_sum, axis=0, keepdims=True), (8, D))
    gains_ref[:, D:] = jnp.broadcast_to(jnp.sum(key_sum_ref[...], axis=0, keepdims=True), (8, D))


def finish_kernel(own_ref, other_ref, k_raw, gain_ref, table_own, dk_ref, dv_ref):
    total = own_ref[...] + other_ref[...].astype(F32)
    unit, inverse = unit_of(k_raw[...])
    back = rotate_back(total[:, :D], *unfold(table_own[...]))
    scaled = back * gain_ref[1:2, :]
    mean = jnp.mean(scaled * unit, axis=1, keepdims=True)
    dk_ref[...] = (inverse * (scaled - unit * mean)).astype(BF16)
    dv_ref[...] = total[:, D:].astype(BF16)


def call_prep(token, lengths, freq, q_raw, dout, both_gains, seq, **kw):
    tokens_own, width = q_raw.shape
    heads = width // D
    rows = heads * tokens_own
    shapes = [
        ((seq, D), F32), ((tokens_own, D), F32),
        ((rows, D), BF16), ((rows, D), BF16),
    ]
    return pl.pallas_call(
        functools.partial(prep_kernel, heads),
        out_shape=[jax.ShapeDtypeStruct(s, t) for s, t in shapes],
        in_specs=[SM, SM, VM, VM, VM, VM],
        out_specs=[VM] * len(shapes),
        scratch_shapes=[pltpu.VMEM((D, D), F32)],
        compiler_params=pltpu.CompilerParams(vmem_limit_bytes=12 * 2**20),
        cost_estimate=pl.CostEstimate(flops=40_000_000, bytes_accessed=4_000_000, transcendentals=0),
        name="prep",
        **kw,
    )(token, lengths, freq, q_raw, dout, both_gains)


def call_attend(token, lengths, kv_own, kv_other, table, q_rows, do_rows, both_gains, **kw):
    tokens_own = kv_own.shape[1]
    heads = q_rows.shape[0] // tokens_own
    width = heads * D
    blocks = kv_own.shape[0] // 2
    kb = 4 * tokens_own
    rows = heads * tokens_own
    shapes = [
        ((tokens_own, width), BF16), ((D, rows), F32), ((2 * blocks, kb // 2, 2 * D), BF16), ((8, D), F32),
    ]
    scratch = [
        pltpu.VMEM((blocks, kb, rows), F32),
        pltpu.VMEM((blocks, kb, D), BF16), pltpu.VMEM((blocks, D, kb), BF16),
        pltpu.VMEM((blocks, D, kb), BF16), pltpu.VMEM((D, rows), F32),
        pltpu.VMEM((8, rows), F32), pltpu.VMEM((8, rows), F32), pltpu.VMEM((8, rows), F32),
        pltpu.VMEM((8, D), F32),
    ]
    return pl.pallas_call(
        functools.partial(attend_kernel, heads),
        out_shape=[jax.ShapeDtypeStruct(s, t) for s, t in shapes],
        in_specs=[SM, SM] + [VM] * 6,
        out_specs=[VM] * len(shapes),
        scratch_shapes=scratch,
        compiler_params=pltpu.CompilerParams(vmem_limit_bytes=20 * 2**20),
        cost_estimate=pl.CostEstimate(flops=3_200_000_000, bytes_accessed=8_000_000, transcendentals=2_000_000),
        name="attend",
        **kw,
    )(token, lengths, kv_own, kv_other, table, q_rows, do_rows, both_gains)


def call_query(dqt, key_sum, table_own, q_raw, both_gains, **kw):
    heads = q_raw.shape[1] // D
    return pl.pallas_call(
        functools.partial(query_kernel, heads),
        out_shape=[jax.ShapeDtypeStruct(q_raw.shape, BF16), jax.ShapeDtypeStruct((8, 2 * D), F32)],
        in_specs=[VM] * 5,
        out_specs=[VM] * 2,
        compiler_params=pltpu.CompilerParams(vmem_limit_bytes=12 * 2**20),
        cost_estimate=pl.CostEstimate(flops=5_000_000, bytes_accessed=2_000_000, transcendentals=0),
        name="query",
        **kw,
    )(dqt, key_sum, table_own, q_raw, both_gains)


def call_finish(own, other, k_raw, both_gains, table_own, **kw):
    shape = jax.ShapeDtypeStruct(k_raw.shape, BF16)
    return pl.pallas_call(
        finish_kernel,
        out_shape=[shape, shape],
        in_specs=[VM] * 5,
        out_specs=[VM] * 2,
        cost_estimate=pl.CostEstimate(flops=0, bytes_accessed=100_000_000, transcendentals=0),
        name="finish",
        **kw,
    )(own, other, k_raw, both_gains, table_own)


def frequency_row():
    exponent = jnp.arange(D // 2, dtype=F32) * (2.0 / D)
    frequency = jnp.power(F32(rope_theta), -exponent)
    return jnp.concatenate([frequency, frequency])[None, :]


def strided(size, stride, count):
    span = stride * count
    return [
        [base + low + stride * k for k in range(count)]
        for base in range(0, size, span)
        for low in range(stride)
    ]


def body(query_raw, key_raw, values, out_grad, doc_lengths, query_gain, key_gain):
    tokens_own = query_raw.shape[1]
    ctx = lax.axis_size("ctx")
    dp = lax.axis_size("dp")
    seq = tokens_own * ctx
    half = ctx // 2
    me = lax.axis_index("ctx")
    token = (me * tokens_own)[None].astype(jnp.int32)
    both_gains = jnp.stack([query_gain, key_gain] * 4)
    columns = [[2 * y + z for y in range(half)] for z in range(2)]
    swap = [(i, i ^ 1) for i in range(ctx)]

    def exchange(blocks):
        return lax.all_to_all(blocks, "ctx", 0, 0, axis_index_groups=columns)

    def spread(rows):
        return jnp.broadcast_to(rows[None], (half,) + rows.shape)

    kv = jnp.concatenate([key_raw[0], values[0]], axis=1)
    kv_swapped = lax.ppermute(kv, "ctx", swap)
    kv_own = exchange(spread(kv))
    kv_other = exchange(spread(kv_swapped))
    table, table_own, q_rows, do_rows = call_prep(token, doc_lengths, frequency_row(), query_raw[0], out_grad[0], both_gains, seq)
    output, dqt, parts, key_sum = call_attend(
        token, doc_lengths, kv_own, kv_other, table, q_rows, do_rows, both_gains
    )
    received = exchange(parts)
    dq, gains = call_query(dqt, key_sum, table_own, query_raw[0], both_gains)
    own = jnp.sum(received[:, :tokens_own].astype(F32), axis=0)
    theirs = jnp.sum(received[:, tokens_own:].astype(F32), axis=0).astype(BF16)
    gains = lax.psum(gains[0], "dp", axis_index_groups=strided(dp, 1, 2))
    gains = lax.psum(gains, "dp", axis_index_groups=strided(dp, 8, dp // 8))
    gains = lax.psum(gains, "ctx", axis_index_groups=strided(ctx, 1, 2))
    other = lax.ppermute(theirs, "ctx", swap)
    own, gains = lax.optimization_barrier((own, gains))
    groups = [
        [(8 * x + 2 * z + core) * ctx + 2 * y + side for z in range(4) for y in range(half)]
        for x in range(dp // 8) for core in range(2) for side in range(2)
    ]
    gains = lax.all_to_all(
        jnp.broadcast_to(gains[None, None], (4 * half, 1, 2 * D)), ("dp", "ctx"), 0, 0, axis_index_groups=groups
    )
    gains = jnp.sum(gains, axis=(0, 1))
    dk, dv = call_finish(own, other, key_raw[0], both_gains, table_own)
    return (output[None], dq[None], dk[None], dv[None], gains[:D], gains[D:])


def solution(mesh):
    return jax.shard_map(
        body,
        mesh=mesh,
        in_specs=(
            P("dp", "ctx", None),
            P("dp", "ctx", None),
            P("dp", "ctx", None),
            P("dp", "ctx", None),
            P("dp", None),
            P(),
            P(),
        ),
        out_specs=(
            P("dp", "ctx", None),
            P("dp", "ctx", None),
            P("dp", "ctx", None),
            P("dp", "ctx", None),
            P(),
            P(),
        ),
        check_vma=False,
    )
```

```python
import functools
import math

import jax
import jax.numpy as jnp
from jax import lax
from jax.experimental import pallas as pl
from jax.experimental.pallas import tpu as pltpu
from jax.sharding import PartitionSpec as P

rope_theta = 1000000.0
norm_epsilon = 1e-06
masked_value = -1e30
D = 128
F32 = jnp.float32
BF16 = jnp.bfloat16
VM = pl.BlockSpec(memory_space=pltpu.VMEM)
SM = pl.BlockSpec(memory_space=pltpu.SMEM)
SCALE = D ** (-0.5)
LOG2E = math.log2(math.e)


def dot(a, b):
    return jnp.dot(a, b, preferred_element_type=F32)


def dot_rows(a, b):
    return lax.dot_general(a, b, (((1,), (1,)), ((), ())), preferred_element_type=F32)


def sin_cos(angle):
    turns = jnp.floor(angle * (2.0 / math.pi) + 0.5)
    r = angle - turns * 1.5703125
    r = r - turns * 4.837512969970703125e-4
    r = r - turns * 7.549789948768648e-8
    r2 = r * r
    s = r + r * r2 * (-1.6666654611e-1 + r2 * (8.3321608736e-3 + r2 * -1.9515295891e-4))
    c = 1.0 - 0.5 * r2 + r2 * r2 * (
        4.166664568298827e-2 + r2 * (-1.388731625493765e-3 + r2 * 2.443315711809948e-5)
    )
    quarter = turns.astype(jnp.int32)
    odd = (quarter & 1) == 1
    sin_part = jnp.where(odd, c, s)
    cos_part = jnp.where(odd, s, c)
    sin_part = jnp.where((quarter & 2) == 2, -sin_part, sin_part)
    cos_part = jnp.where(((quarter + 1) & 2) == 2, -cos_part, cos_part)
    return sin_part, cos_part


def starts_of(lengths, tokens):
    end = jnp.int32(0)
    start = jnp.zeros_like(tokens)
    for d in range(lengths.shape[1]):
        end = end + lengths[0, d]
        start = jnp.where(tokens >= end, end, start)
    return start


def unfold(table):
    turned = pltpu.roll(table, D // 2, 1)
    first_lanes = lax.broadcasted_iota(jnp.int32, table.shape, 1) < D // 2
    return jnp.where(first_lanes, table, turned), jnp.where(first_lanes, -turned, table)


def rotate(x, cosine, sine):
    return x * cosine + pltpu.roll(x, D // 2, 1) * sine


def rotate_back(x, cosine, sine):
    return x * cosine - pltpu.roll(x, D // 2, 1) * sine


def unit_of(raw):
    x = raw.astype(F32)
    inverse = lax.rsqrt(jnp.mean(x * x, axis=1, keepdims=True) + norm_epsilon)
    return x * inverse, inverse


def prep_kernel(
    heads, token_ref, lengths, freq, q_raw, dout, gain_ref,
    table_ref, table_own, q_ref, do_ref, pos_ref,
):
    tokens_own = q_raw.shape[0]
    seq = table_ref.shape[0]
    row = lax.broadcasted_iota(jnp.int32, (D, D), 0)
    lane = lax.broadcasted_iota(jnp.int32, (D, D), 1)
    tokens = row * D + lane
    positions = tokens - starts_of(lengths, tokens)
    pos_ref[...] = positions.astype(F32).T
    first_lanes = lane < D // 2
    for i in range(seq // D):
        angle = pos_ref[:, i : i + 1] * freq[...]
        s, c = sin_cos(angle)
        table_ref[i * D : (i + 1) * D, :] = jnp.where(first_lanes, c, s)
    first = pl.multiple_of(token_ref[0], tokens_own)
    mine = table_ref[pl.ds(first, tokens_own), :]
    table_own[...] = mine
    cosine, sine = unfold(mine)
    for h in range(heads):
        cols = slice(h * D, (h + 1) * D)
        rows = slice(h * tokens_own, (h + 1) * tokens_own)
        unit, _ = unit_of(q_raw[:, cols])
        q = rotate(unit * gain_ref[0:1, :], cosine, sine)
        q_ref[rows, :] = q.astype(BF16)
        do_ref[rows, :] = dout[:, cols]


def attend_kernel(
    heads, token_ref, lengths, kv_own, kv_other, table_ref, q_ref, do_ref, gain_ref,
    out_ref, dqt_buf, dkv_ref, key_sum_ref,
    s_buf, k_buf, kt_buf, vt_buf, ot_buf, max_buf, sum_buf, row_buf, kg_buf,
):
    _, tokens_own, _ = kv_own.shape
    kb = 4 * tokens_own
    blocks = kv_own.shape[0] // 2
    cols_all = heads * tokens_own
    cc = cols_all
    chunks = cols_all // cc
    first = token_ref[0]
    end = jnp.int32(0)
    low = jnp.int32(0)
    for d in range(lengths.shape[1]):
        end = end + lengths[0, d]
        low = jnp.where(end <= first, end, low)
    lo = low // kb
    hi = (first + tokens_own - 1) // kb + 1
    tok = first + lax.broadcasted_iota(jnp.int32, (8, tokens_own), 1)
    start_row = starts_of(lengths, tok)[:1]
    tok_row = tok[:1]
    dkv_ref[...] = jnp.zeros_like(dkv_ref)
    max_buf[...] = jnp.full_like(max_buf, masked_value)
    sum_buf[...] = jnp.zeros_like(sum_buf)
    ot_buf[...] = jnp.zeros_like(ot_buf)
    dqt_buf[...] = jnp.zeros_like(dqt_buf)
    kg_buf[...] = jnp.zeros_like(kg_buf)
    factor = SCALE * LOG2E

    side = (first // tokens_own) % 2

    def tables(b):
        rows = []
        for i in range(2):
            for s in (side, 1 - side):
                start = b * kb + (2 * i + s) * tokens_own
                rows.append(table_ref[pl.ds(pl.multiple_of(start, tokens_own), tokens_own), :])
        return unfold(jnp.concatenate(rows, 0))

    def keys_of(b):
        return jnp.concatenate([kv_own[2 * b, :, :D], kv_other[2 * b, :, :D], kv_own[2 * b + 1, :, :D], kv_other[2 * b + 1, :, :D]], 0)

    def values_of(b):
        return jnp.concatenate([kv_own[2 * b, :, D:], kv_other[2 * b, :, D:], kv_own[2 * b + 1, :, D:], kv_other[2 * b + 1, :, D:]], 0)

    row = lax.broadcasted_iota(jnp.int32, (kb, tokens_own), 0)
    key_shift = row + jnp.where(row % (2 * tokens_own) < tokens_own, side * tokens_own, -side * tokens_own)

    def prepare(b):
        unit, _ = unit_of(keys_of(b))
        k = rotate(unit * gain_ref[1:2, :], *tables(b))
        k_buf[b] = k.astype(BF16)
        kt_buf[b] = k.T.astype(BF16)
        vt_buf[b] = values_of(b).astype(F32).T.astype(BF16)

    def scores_step(b, carry):
        key = b * kb + key_shift
        allowed = (key >= start_row) & (key <= tok_row)
        bias = jnp.where(allowed, 0.0, masked_value)
        for c in range(chunks):
            cs = slice(c * cc, (c + 1) * cc)
            s = dot_rows(k_buf[b], q_ref[cs, :]) * factor + jnp.concatenate([bias] * (cc // tokens_own), 1)
            s_buf[b, :, cs] = s
            max_buf[:, cs] = jnp.maximum(max_buf[:, cs], jnp.max(s.reshape(kb // 8, 8, cc), axis=0))
        prepare(jnp.minimum(b + 1, blocks - 1))
        return carry

    prepare(lo)
    lax.fori_loop(lo, hi, scores_step, 0)
    row_buf[:1, :] = jnp.max(max_buf[...], axis=0, keepdims=True)

    def exp_step(b, carry):
        for c in range(chunks):
            cs = slice(c * cc, (c + 1) * cc)
            e = jnp.exp2(s_buf[b, :, cs] - row_buf[:1, cs])
            s_buf[b, :, cs] = e
            sum_buf[:, cs] += jnp.sum(e.reshape(kb // 8, 8, cc), axis=0)
            ot_buf[:, cs] += dot(vt_buf[b], e.astype(BF16))
        return carry

    lax.fori_loop(lo, hi, exp_step, 0)
    sum_buf[:1, :] = 1.0 / jnp.sum(sum_buf[...], axis=0, keepdims=True)
    for h in range(heads):
        hs = slice(h * tokens_own, (h + 1) * tokens_own)
        ot = (ot_buf[:, hs] * sum_buf[:1, hs]).astype(BF16).astype(F32)
        out_ref[:, h * D : (h + 1) * D] = ot.T.astype(BF16)
        row_buf[:1, hs] = jnp.sum(ot * do_ref[hs, :].T.astype(F32), axis=0, keepdims=True)

    def back_step(b, carry):
        dk = jnp.zeros((kb, D), F32)
        dv = jnp.zeros((kb, D), F32)
        v_rows = values_of(b)
        for c in range(chunks):
            cs = slice(c * cc, (c + 1) * cc)
            dp = dot_rows(v_rows, do_ref[cs, :])
            prob = s_buf[b, :, cs] * sum_buf[:1, cs]
            dv = dv + dot(prob.astype(BF16), do_ref[cs, :])
            ds = (prob * (dp - row_buf[:1, cs])).astype(BF16)
            dk = dk + dot(ds, q_ref[cs, :])
            dqt_buf[:, cs] += dot(kt_buf[b], ds)
        dk = dk * SCALE
        for i in range(2):
            half = slice(i * 2 * tokens_own, (i + 1) * 2 * tokens_own)
            dkv_ref[2 * b + i, :, :D] = dk[half].astype(BF16)
            dkv_ref[2 * b + i, :, D:] = dv[half].astype(BF16)
        unit, _ = unit_of(keys_of(b))
        terms = rotate_back(dk, *tables(b)) * unit
        kg_buf[...] += jnp.sum(terms.reshape(kb // 8, 8, D), axis=0)
        return carry

    lax.fori_loop(lo, hi, back_step, 0)
    key_sum_ref[...] = kg_buf[...]


def query_kernel(heads, dqt_ref, key_sum_ref, table_own, q_raw, gain_ref, dq_ref, gains_ref):
    tokens_own = q_raw.shape[0]
    cosine, sine = unfold(table_own[...])
    q_sum = jnp.zeros((8, D), F32)
    for h in range(heads):
        hs = slice(h * tokens_own, (h + 1) * tokens_own)
        back = rotate_back(dqt_ref[:, hs].T * SCALE, cosine, sine)
        unit, inverse = unit_of(q_raw[:, h * D : (h + 1) * D])
        q_sum = q_sum + jnp.sum((back * unit).reshape(tokens_own // 8, 8, D), axis=0)
        scaled = back * gain_ref[0:1, :]
        mean = jnp.mean(scaled * unit, axis=1, keepdims=True)
        dq_ref[:, h * D : (h + 1) * D] = (inverse * (scaled - unit * mean)).astype(BF16)
    gains_ref[:, :D] = jnp.broadcast_to(jnp.sum(q_sum, axis=0, keepdims=True), (8, D))
    gains_ref[:, D:] = jnp.broadcast_to(jnp.sum(key_sum_ref[...], axis=0, keepdims=True), (8, D))


def finish_kernel(own_ref, other_ref, k_raw, gain_ref, table_own, dk_ref, dv_ref):
    total = own_ref[...] + other_ref[...].astype(F32)
    unit, inverse = unit_of(k_raw[...])
    back = rotate_back(total[:, :D], *unfold(table_own[...]))
    scaled = back * gain_ref[1:2, :]
    mean = jnp.mean(scaled * unit, axis=1, keepdims=True)
    dk_ref[...] = (inverse * (scaled - unit * mean)).astype(BF16)
    dv_ref[...] = total[:, D:].astype(BF16)


def call_prep(token, lengths, freq, q_raw, dout, both_gains, seq, **kw):
    tokens_own, width = q_raw.shape
    heads = width // D
    rows = heads * tokens_own
    shapes = [
        ((seq, D), F32), ((tokens_own, D), F32),
        ((rows, D), BF16), ((rows, D), BF16),
    ]
    return pl.pallas_call(
        functools.partial(prep_kernel, heads),
        out_shape=[jax.ShapeDtypeStruct(s, t) for s, t in shapes],
        in_specs=[SM, SM, VM, VM, VM, VM],
        out_specs=[VM] * len(shapes),
        scratch_shapes=[pltpu.VMEM((D, D), F32)],
        compiler_params=pltpu.CompilerParams(vmem_limit_bytes=12 * 2**20),
        cost_estimate=pl.CostEstimate(flops=40_000_000, bytes_accessed=4_000_000, transcendentals=0),
        name="prep",
        **kw,
    )(token, lengths, freq, q_raw, dout, both_gains)


def call_attend(token, lengths, kv_own, kv_other, table, q_rows, do_rows, both_gains, **kw):
    tokens_own = kv_own.shape[1]
    heads = q_rows.shape[0] // tokens_own
    width = heads * D
    blocks = kv_own.shape[0] // 2
    kb = 4 * tokens_own
    rows = heads * tokens_own
    shapes = [
        ((tokens_own, width), BF16), ((D, rows), F32), ((2 * blocks, kb // 2, 2 * D), BF16), ((8, D), F32),
    ]
    scratch = [
        pltpu.VMEM((blocks, kb, rows), F32),
        pltpu.VMEM((blocks, kb, D), BF16), pltpu.VMEM((blocks, D, kb), BF16),
        pltpu.VMEM((blocks, D, kb), BF16), pltpu.VMEM((D, rows), F32),
        pltpu.VMEM((8, rows), F32), pltpu.VMEM((8, rows), F32), pltpu.VMEM((8, rows), F32),
        pltpu.VMEM((8, D), F32),
    ]
    return pl.pallas_call(
        functools.partial(attend_kernel, heads),
        out_shape=[jax.ShapeDtypeStruct(s, t) for s, t in shapes],
        in_specs=[SM, SM] + [VM] * 6,
        out_specs=[VM] * len(shapes),
        scratch_shapes=scratch,
        compiler_params=pltpu.CompilerParams(vmem_limit_bytes=20 * 2**20),
        cost_estimate=pl.CostEstimate(flops=3_200_000_000, bytes_accessed=8_000_000, transcendentals=2_000_000),
        name="attend",
        **kw,
    )(token, lengths, kv_own, kv_other, table, q_rows, do_rows, both_gains)


def call_query(dqt, key_sum, table_own, q_raw, both_gains, **kw):
    heads = q_raw.shape[1] // D
    return pl.pallas_call(
        functools.partial(query_kernel, heads),
        out_shape=[jax.ShapeDtypeStruct(q_raw.shape, BF16), jax.ShapeDtypeStruct((8, 2 * D), F32)],
        in_specs=[VM] * 5,
        out_specs=[VM] * 2,
        compiler_params=pltpu.CompilerParams(vmem_limit_bytes=12 * 2**20),
        cost_estimate=pl.CostEstimate(flops=5_000_000, bytes_accessed=2_000_000, transcendentals=0),
        name="query",
        **kw,
    )(dqt, key_sum, table_own, q_raw, both_gains)


def call_finish(own, other, k_raw, both_gains, table_own, **kw):
    shape = jax.ShapeDtypeStruct(k_raw.shape, BF16)
    return pl.pallas_call(
        finish_kernel,
        out_shape=[shape, shape],
        in_specs=[VM] * 5,
        out_specs=[VM] * 2,
        compiler_params=pltpu.CompilerParams(vmem_limit_bytes=4 * 2**20),
        cost_estimate=pl.CostEstimate(flops=1_000_000, bytes_accessed=500_000, transcendentals=0),
        name="finish",
        **kw,
    )(own, other, k_raw, both_gains, table_own)


def frequency_row():
    exponent = jnp.arange(D // 2, dtype=F32) * (2.0 / D)
    frequency = jnp.power(F32(rope_theta), -exponent)
    return jnp.concatenate([frequency, frequency])[None, :]


def strided(size, stride, count):
    span = stride * count
    return [
        [base + low + stride * k for k in range(count)]
        for base in range(0, size, span)
        for low in range(stride)
    ]


def body(query_raw, key_raw, values, out_grad, doc_lengths, query_gain, key_gain):
    tokens_own = query_raw.shape[1]
    ctx = lax.axis_size("ctx")
    dp = lax.axis_size("dp")
    seq = tokens_own * ctx
    half = ctx // 2
    me = lax.axis_index("ctx")
    token = (me * tokens_own)[None].astype(jnp.int32)
    both_gains = jnp.stack([query_gain, key_gain] * 4)
    columns = [[2 * y + z for y in range(half)] for z in range(2)]
    swap = [(i, i ^ 1) for i in range(ctx)]

    def exchange(blocks):
        return lax.all_to_all(blocks, "ctx", 0, 0, axis_index_groups=columns)

    def spread(rows):
        return jnp.broadcast_to(rows[None], (half,) + rows.shape)

    kv = jnp.concatenate([key_raw[0], values[0]], axis=1)
    kv_swapped = lax.ppermute(kv, "ctx", swap)
    kv_own = exchange(
        jnp.concatenate([spread(key_raw[0]), spread(values[0])], axis=2)
    )
    kv_other = exchange(spread(kv_swapped))
    table, table_own, q_rows, do_rows = call_prep(token, doc_lengths, frequency_row(), query_raw[0], out_grad[0], both_gains, seq)
    output, dqt, parts, key_sum = call_attend(
        token, doc_lengths, kv_own, kv_other, table, q_rows, do_rows, both_gains
    )
    received = exchange(parts)
    dq, gains = call_query(dqt, key_sum, table_own, query_raw[0], both_gains)
    own = jnp.sum(received[:, :tokens_own].astype(F32), axis=0)
    theirs = jnp.sum(received[:, tokens_own:].astype(F32), axis=0).astype(BF16)
    def flat(x, y, z, core):
        return ((x * 4 + z % 4) * 2 + core) * ctx + 2 * y + z // 4

    xs, ys, zs, cores = range(dp // 8), range(half), range(8), range(2)
    along_z = [[flat(x, y, z, core) for z in zs] for x in xs for y in ys for core in cores]
    along_xy = [[flat(x, y, z, core) for x in xs for y in ys] for z in zs for core in cores]
    gains = lax.psum(gains[0], "dp", axis_index_groups=strided(dp, 1, 2))
    gains = lax.psum(gains, ("dp", "ctx"), axis_index_groups=along_z)
    theirs, gains = lax.optimization_barrier((theirs, gains))
    other = lax.ppermute(theirs, "ctx", swap)
    gains = lax.all_to_all(
        jnp.broadcast_to(gains[None, None], (len(along_xy[0]), 1, 2 * D)), ("dp", "ctx"), 0, 0, axis_index_groups=along_xy
    )
    gains = jnp.sum(gains, axis=(0, 1))
    dk, dv = call_finish(own, other, key_raw[0], both_gains, table_own)
    return (output[None], dq[None], dk[None], dv[None], gains[:D], gains[D:])


def solution(mesh):
    return jax.shard_map(
        body,
        mesh=mesh,
        in_specs=(
            P("dp", "ctx", None),
            P("dp", "ctx", None),
            P("dp", "ctx", None),
            P("dp", "ctx", None),
            P("dp", None),
            P(),
            P(),
        ),
        out_specs=(
            P("dp", "ctx", None),
            P("dp", "ctx", None),
            P("dp", "ctx", None),
            P("dp", "ctx", None),
            P(),
            P(),
        ),
        check_vma=False,
    )
```

```python
import functools
import math

import jax
import jax.numpy as jnp
from jax import lax
from jax.experimental import pallas as pl
from jax.experimental.pallas import tpu as pltpu
from jax.sharding import PartitionSpec as P

rope_theta = 1000000.0
norm_epsilon = 1e-06
masked_value = -1e30
D = 128
F32 = jnp.float32
BF16 = jnp.bfloat16
VM = pl.BlockSpec(memory_space=pltpu.VMEM)
SM = pl.BlockSpec(memory_space=pltpu.SMEM)
SCALE = D ** (-0.5)
LOG2E = math.log2(math.e)


def dot(a, b):
    return jnp.dot(a, b, preferred_element_type=F32)


def dot_rows(a, b):
    return lax.dot_general(a, b, (((1,), (1,)), ((), ())), preferred_element_type=F32)


def sin_cos(angle):
    turns = jnp.floor(angle * (2.0 / math.pi) + 0.5)
    r = angle - turns * 1.5703125
    r = r - turns * 4.837512969970703125e-4
    r = r - turns * 7.549789948768648e-8
    r2 = r * r
    s = r + r * r2 * (-1.6666654611e-1 + r2 * (8.3321608736e-3 + r2 * -1.9515295891e-4))
    c = 1.0 - 0.5 * r2 + r2 * r2 * (
        4.166664568298827e-2 + r2 * (-1.388731625493765e-3 + r2 * 2.443315711809948e-5)
    )
    quarter = turns.astype(jnp.int32)
    odd = (quarter & 1) == 1
    sin_part = jnp.where(odd, c, s)
    cos_part = jnp.where(odd, s, c)
    sin_part = jnp.where((quarter & 2) == 2, -sin_part, sin_part)
    cos_part = jnp.where(((quarter + 1) & 2) == 2, -cos_part, cos_part)
    return sin_part, cos_part


def starts_of(lengths, tokens):
    end = jnp.int32(0)
    start = jnp.zeros_like(tokens)
    for d in range(lengths.shape[1]):
        end = end + lengths[0, d]
        start = jnp.where(tokens >= end, end, start)
    return start


def unfold(table):
    turned = pltpu.roll(table, D // 2, 1)
    first_lanes = lax.broadcasted_iota(jnp.int32, table.shape, 1) < D // 2
    return jnp.where(first_lanes, table, turned), jnp.where(first_lanes, -turned, table)


def rotate(x, cosine, sine):
    return x * cosine + pltpu.roll(x, D // 2, 1) * sine


def rotate_back(x, cosine, sine):
    return x * cosine - pltpu.roll(x, D // 2, 1) * sine


def unit_of(raw):
    x = raw.astype(F32)
    inverse = lax.rsqrt(jnp.mean(x * x, axis=1, keepdims=True) + norm_epsilon)
    return x * inverse, inverse


def prep_kernel(
    heads, token_ref, lengths, freq, q_raw, dout, gain_ref,
    table_ref, table_own, q_ref, do_ref, pos_ref,
):
    tokens_own = q_raw.shape[0]
    seq = table_ref.shape[0]
    row = lax.broadcasted_iota(jnp.int32, (D, D), 0)
    lane = lax.broadcasted_iota(jnp.int32, (D, D), 1)
    tokens = row * D + lane
    positions = tokens - starts_of(lengths, tokens)
    pos_ref[...] = positions.astype(F32).T
    first_lanes = lane < D // 2
    for i in range(seq // D):
        angle = pos_ref[:, i : i + 1] * freq[...]
        s, c = sin_cos(angle)
        table_ref[i * D : (i + 1) * D, :] = jnp.where(first_lanes, c, s)
    first = pl.multiple_of(token_ref[0], tokens_own)
    mine = table_ref[pl.ds(first, tokens_own), :]
    table_own[...] = mine
    cosine, sine = unfold(mine)
    for h in range(heads):
        cols = slice(h * D, (h + 1) * D)
        rows = slice(h * tokens_own, (h + 1) * tokens_own)
        unit, _ = unit_of(q_raw[:, cols])
        q = rotate(unit * gain_ref[0:1, :], cosine, sine)
        q_ref[rows, :] = q.astype(BF16)
        do_ref[rows, :] = dout[:, cols]


def attend_kernel(
    heads, token_ref, lengths, kv_own, kv_other, table_ref, q_ref, do_ref, gain_ref,
    out_ref, dqt_buf, dkv_ref, key_sum_ref,
    s_buf, k_buf, kt_buf, vt_buf, ot_buf, max_buf, sum_buf, row_buf, kg_buf,
):
    _, tokens_own, _ = kv_own.shape
    kb = 4 * tokens_own
    blocks = kv_own.shape[0] // 2
    cols_all = heads * tokens_own
    cc = cols_all
    chunks = cols_all // cc
    first = token_ref[0]
    end = jnp.int32(0)
    low = jnp.int32(0)
    for d in range(lengths.shape[1]):
        end = end + lengths[0, d]
        low = jnp.where(end <= first, end, low)
    lo = low // kb
    hi = (first + tokens_own - 1) // kb + 1
    tok = first + lax.broadcasted_iota(jnp.int32, (8, tokens_own), 1)
    start_row = starts_of(lengths, tok)[:1]
    tok_row = tok[:1]
    dkv_ref[...] = jnp.zeros_like(dkv_ref)
    max_buf[...] = jnp.full_like(max_buf, masked_value)
    sum_buf[...] = jnp.zeros_like(sum_buf)
    ot_buf[...] = jnp.zeros_like(ot_buf)
    dqt_buf[...] = jnp.zeros_like(dqt_buf)
    kg_buf[...] = jnp.zeros_like(kg_buf)
    factor = SCALE * LOG2E

    side = (first // tokens_own) % 2

    def tables(b):
        rows = []
        for i in range(2):
            for s in (side, 1 - side):
                start = b * kb + (2 * i + s) * tokens_own
                rows.append(table_ref[pl.ds(pl.multiple_of(start, tokens_own), tokens_own), :])
        return unfold(jnp.concatenate(rows, 0))

    def keys_of(b):
        return jnp.concatenate([kv_own[2 * b, :, :D], kv_other[2 * b, :, :D], kv_own[2 * b + 1, :, :D], kv_other[2 * b + 1, :, :D]], 0)

    def values_of(b):
        return jnp.concatenate([kv_own[2 * b, :, D:], kv_other[2 * b, :, D:], kv_own[2 * b + 1, :, D:], kv_other[2 * b + 1, :, D:]], 0)

    row = lax.broadcasted_iota(jnp.int32, (kb, tokens_own), 0)
    key_shift = row + jnp.where(row % (2 * tokens_own) < tokens_own, side * tokens_own, -side * tokens_own)

    def prepare(b):
        unit, _ = unit_of(keys_of(b))
        k = rotate(unit * gain_ref[1:2, :], *tables(b))
        k_buf[b] = k.astype(BF16)
        kt_buf[b] = k.T.astype(BF16)
        vt_buf[b] = values_of(b).astype(F32).T.astype(BF16)

    def scores_step(b, carry):
        key = b * kb + key_shift
        allowed = (key >= start_row) & (key <= tok_row)
        bias = jnp.where(allowed, 0.0, masked_value)
        for c in range(chunks):
            cs = slice(c * cc, (c + 1) * cc)
            s = dot_rows(k_buf[b], q_ref[cs, :]) * factor + jnp.concatenate([bias] * (cc // tokens_own), 1)
            s_buf[b, :, cs] = s
            max_buf[:, cs] = jnp.maximum(max_buf[:, cs], jnp.max(s.reshape(kb // 8, 8, cc), axis=0))
        prepare(jnp.minimum(b + 1, blocks - 1))
        return carry

    prepare(lo)
    lax.fori_loop(lo, hi, scores_step, 0)
    row_buf[:1, :] = jnp.max(max_buf[...], axis=0, keepdims=True)

    def exp_step(b, carry):
        for c in range(chunks):
            cs = slice(c * cc, (c + 1) * cc)
            e = jnp.exp2(s_buf[b, :, cs] - row_buf[:1, cs])
            s_buf[b, :, cs] = e
            sum_buf[:, cs] += jnp.sum(e.reshape(kb // 8, 8, cc), axis=0)
            ot_buf[:, cs] += dot(vt_buf[b], e.astype(BF16))
        return carry

    lax.fori_loop(lo, hi, exp_step, 0)
    sum_buf[:1, :] = 1.0 / jnp.sum(sum_buf[...], axis=0, keepdims=True)
    for h in range(heads):
        hs = slice(h * tokens_own, (h + 1) * tokens_own)
        ot = (ot_buf[:, hs] * sum_buf[:1, hs]).astype(BF16).astype(F32)
        out_ref[:, h * D : (h + 1) * D] = ot.T.astype(BF16)
        row_buf[:1, hs] = jnp.sum(ot * do_ref[hs, :].T.astype(F32), axis=0, keepdims=True)

    def back_step(b, carry):
        dk = jnp.zeros((kb, D), F32)
        dv = jnp.zeros((kb, D), F32)
        v_rows = values_of(b)
        for c in range(chunks):
            cs = slice(c * cc, (c + 1) * cc)
            dp = dot_rows(v_rows, do_ref[cs, :])
            prob = s_buf[b, :, cs] * sum_buf[:1, cs]
            dv = dv + dot(prob.astype(BF16), do_ref[cs, :])
            ds = (prob * (dp - row_buf[:1, cs])).astype(BF16)
            dk = dk + dot(ds, q_ref[cs, :])
            dqt_buf[:, cs] += dot(kt_buf[b], ds)
        dk = dk * SCALE
        for i in range(2):
            half = slice(i * 2 * tokens_own, (i + 1) * 2 * tokens_own)
            dkv_ref[2 * b + i, :, :D] = dk[half].astype(BF16)
            dkv_ref[2 * b + i, :, D:] = dv[half].astype(BF16)
        unit, _ = unit_of(keys_of(b))
        terms = rotate_back(dk, *tables(b)) * unit
        kg_buf[...] += jnp.sum(terms.reshape(kb // 8, 8, D), axis=0)
        return carry

    lax.fori_loop(lo, hi, back_step, 0)
    key_sum_ref[...] = kg_buf[...]


def query_kernel(heads, dqt_ref, key_sum_ref, table_own, q_raw, gain_ref, dq_ref, gains_ref):
    tokens_own = q_raw.shape[0]
    cosine, sine = unfold(table_own[...])
    q_sum = jnp.zeros((8, D), F32)
    for h in range(heads):
        hs = slice(h * tokens_own, (h + 1) * tokens_own)
        back = rotate_back(dqt_ref[:, hs].T * SCALE, cosine, sine)
        unit, inverse = unit_of(q_raw[:, h * D : (h + 1) * D])
        q_sum = q_sum + jnp.sum((back * unit).reshape(tokens_own // 8, 8, D), axis=0)
        scaled = back * gain_ref[0:1, :]
        mean = jnp.mean(scaled * unit, axis=1, keepdims=True)
        dq_ref[:, h * D : (h + 1) * D] = (inverse * (scaled - unit * mean)).astype(BF16)
    gains_ref[:, :D] = jnp.broadcast_to(jnp.sum(q_sum, axis=0, keepdims=True), (8, D))
    gains_ref[:, D:] = jnp.broadcast_to(jnp.sum(key_sum_ref[...], axis=0, keepdims=True), (8, D))


def copies_kernel(*refs):
    out_ref = refs[-1]
    rows = jnp.concatenate([ref[...] for ref in refs[:-1]], axis=1)
    for i in range(out_ref.shape[0]):
        out_ref[i] = rows


def finish_kernel(own_ref, other_ref, k_raw, gain_ref, table_own, dk_ref, dv_ref):
    total = own_ref[...] + other_ref[...].astype(F32)
    unit, inverse = unit_of(k_raw[...])
    back = rotate_back(total[:, :D], *unfold(table_own[...]))
    scaled = back * gain_ref[1:2, :]
    mean = jnp.mean(scaled * unit, axis=1, keepdims=True)
    dk_ref[...] = (inverse * (scaled - unit * mean)).astype(BF16)
    dv_ref[...] = total[:, D:].astype(BF16)


def call_prep(token, lengths, freq, q_raw, dout, both_gains, seq, **kw):
    tokens_own, width = q_raw.shape
    heads = width // D
    rows = heads * tokens_own
    shapes = [
        ((seq, D), F32), ((tokens_own, D), F32),
        ((rows, D), BF16), ((rows, D), BF16),
    ]
    return pl.pallas_call(
        functools.partial(prep_kernel, heads),
        out_shape=[jax.ShapeDtypeStruct(s, t) for s, t in shapes],
        in_specs=[SM, SM, VM, VM, VM, VM],
        out_specs=[VM] * len(shapes),
        scratch_shapes=[pltpu.VMEM((D, D), F32)],
        compiler_params=pltpu.CompilerParams(vmem_limit_bytes=12 * 2**20),
        cost_estimate=pl.CostEstimate(flops=40_000_000, bytes_accessed=4_000_000, transcendentals=0),
        name="prep",
        **kw,
    )(token, lengths, freq, q_raw, dout, both_gains)


def call_attend(token, lengths, kv_own, kv_other, table, q_rows, do_rows, both_gains, **kw):
    tokens_own = kv_own.shape[1]
    heads = q_rows.shape[0] // tokens_own
    width = heads * D
    blocks = kv_own.shape[0] // 2
    kb = 4 * tokens_own
    rows = heads * tokens_own
    shapes = [
        ((tokens_own, width), BF16), ((D, rows), F32), ((2 * blocks, kb // 2, 2 * D), BF16), ((8, D), F32),
    ]
    scratch = [
        pltpu.VMEM((blocks, kb, rows), F32),
        pltpu.VMEM((blocks, kb, D), BF16), pltpu.VMEM((blocks, D, kb), BF16),
        pltpu.VMEM((blocks, D, kb), BF16), pltpu.VMEM((D, rows), F32),
        pltpu.VMEM((8, rows), F32), pltpu.VMEM((8, rows), F32), pltpu.VMEM((8, rows), F32),
        pltpu.VMEM((8, D), F32),
    ]
    return pl.pallas_call(
        functools.partial(attend_kernel, heads),
        out_shape=[jax.ShapeDtypeStruct(s, t) for s, t in shapes],
        in_specs=[SM, SM] + [VM] * 6,
        out_specs=[VM] * len(shapes),
        scratch_shapes=scratch,
        compiler_params=pltpu.CompilerParams(vmem_limit_bytes=20 * 2**20),
        cost_estimate=pl.CostEstimate(flops=3_200_000_000, bytes_accessed=8_000_000, transcendentals=2_000_000),
        name="attend",
        **kw,
    )(token, lengths, kv_own, kv_other, table, q_rows, do_rows, both_gains)


def call_copies(count, *parts):
    shape = (count, parts[0].shape[0], sum(part.shape[1] for part in parts))
    size = math.prod(shape) * parts[0].dtype.itemsize
    return pl.pallas_call(
        copies_kernel,
        out_shape=jax.ShapeDtypeStruct(shape, parts[0].dtype),
        in_specs=[VM] * len(parts),
        out_specs=VM,
        compiler_params=pltpu.CompilerParams(vmem_limit_bytes=4 * 2**20),
        cost_estimate=pl.CostEstimate(flops=0, bytes_accessed=size, transcendentals=0),
        name="copies",
    )(*parts)


def call_query(dqt, key_sum, table_own, q_raw, both_gains, **kw):
    heads = q_raw.shape[1] // D
    return pl.pallas_call(
        functools.partial(query_kernel, heads),
        out_shape=[jax.ShapeDtypeStruct(q_raw.shape, BF16), jax.ShapeDtypeStruct((8, 2 * D), F32)],
        in_specs=[VM] * 5,
        out_specs=[VM] * 2,
        compiler_params=pltpu.CompilerParams(vmem_limit_bytes=12 * 2**20),
        cost_estimate=pl.CostEstimate(flops=5_000_000, bytes_accessed=2_000_000, transcendentals=0),
        name="query",
        **kw,
    )(dqt, key_sum, table_own, q_raw, both_gains)


def call_finish(own, other, k_raw, both_gains, table_own, **kw):
    shape = jax.ShapeDtypeStruct(k_raw.shape, BF16)
    return pl.pallas_call(
        finish_kernel,
        out_shape=[shape, shape],
        in_specs=[VM] * 5,
        out_specs=[VM] * 2,
        compiler_params=pltpu.CompilerParams(vmem_limit_bytes=4 * 2**20),
        cost_estimate=pl.CostEstimate(flops=1_000_000, bytes_accessed=500_000, transcendentals=0),
        name="finish",
        **kw,
    )(own, other, k_raw, both_gains, table_own)


def frequency_row():
    exponent = jnp.arange(D // 2, dtype=F32) * (2.0 / D)
    frequency = jnp.power(F32(rope_theta), -exponent)
    return jnp.concatenate([frequency, frequency])[None, :]


def strided(size, stride, count):
    span = stride * count
    return [
        [base + low + stride * k for k in range(count)]
        for base in range(0, size, span)
        for low in range(stride)
    ]


def body(query_raw, key_raw, values, out_grad, doc_lengths, query_gain, key_gain):
    tokens_own = query_raw.shape[1]
    ctx = lax.axis_size("ctx")
    dp = lax.axis_size("dp")
    seq = tokens_own * ctx
    half = ctx // 2
    me = lax.axis_index("ctx")
    token = (me * tokens_own)[None].astype(jnp.int32)
    both_gains = jnp.stack([query_gain, key_gain] * 4)
    columns = [[2 * y + z for y in range(half)] for z in range(2)]
    swap = [(i, i ^ 1) for i in range(ctx)]

    def exchange(blocks):
        return lax.all_to_all(blocks, "ctx", 0, 0, axis_index_groups=columns)

    def spread(rows):
        return jnp.broadcast_to(rows[None], (half,) + rows.shape)

    kv = jnp.concatenate([key_raw[0], values[0]], axis=1)
    kv_swapped = lax.ppermute(kv, "ctx", swap)
    kv_own = exchange(
        jnp.concatenate([spread(key_raw[0]), spread(values[0])], axis=2)
    )
    kv_other = exchange(call_copies(half, kv_swapped))
    table, table_own, q_rows, do_rows = call_prep(token, doc_lengths, frequency_row(), query_raw[0], out_grad[0], both_gains, seq)
    output, dqt, parts, key_sum = call_attend(
        token, doc_lengths, kv_own, kv_other, table, q_rows, do_rows, both_gains
    )
    received = exchange(parts)
    dq, gains = call_query(dqt, key_sum, table_own, query_raw[0], both_gains)
    own = jnp.sum(received[:, :tokens_own].astype(F32), axis=0)
    theirs = jnp.sum(received[:, tokens_own:].astype(F32), axis=0).astype(BF16)
    def flat(x, y, z, core):
        return ((x * 4 + z % 4) * 2 + core) * ctx + 2 * y + z // 4

    xs, ys, zs, cores = range(dp // 8), range(half), range(8), range(2)
    along_z = [[flat(x, y, z, core) for z in zs] for x in xs for y in ys for core in cores]
    along_xy = [[flat(x, y, z, core) for x in xs for y in ys] for z in zs for core in cores]
    gains = lax.psum(gains[0], "dp", axis_index_groups=strided(dp, 1, 2))
    gains = lax.psum(gains, ("dp", "ctx"), axis_index_groups=along_z)
    copies = call_copies(len(along_xy[0]), gains[None])
    theirs, copies = lax.optimization_barrier((theirs, copies))
    other = lax.ppermute(theirs, "ctx", swap)
    gains = lax.all_to_all(copies, ("dp", "ctx"), 0, 0, axis_index_groups=along_xy)
    gains = jnp.sum(gains, axis=(0, 1))
    dk, dv = call_finish(own, other, key_raw[0], both_gains, table_own)
    return (output[None], dq[None], dk[None], dv[None], gains[:D], gains[D:])


def solution(mesh):
    return jax.shard_map(
        body,
        mesh=mesh,
        in_specs=(
            P("dp", "ctx", None),
            P("dp", "ctx", None),
            P("dp", "ctx", None),
            P("dp", "ctx", None),
            P("dp", None),
            P(),
            P(),
        ),
        out_specs=(
            P("dp", "ctx", None),
            P("dp", "ctx", None),
            P("dp", "ctx", None),
            P("dp", "ctx", None),
            P(),
            P(),
        ),
        check_vma=False,
    )
```

```python
import functools
import math

import jax
import jax.numpy as jnp
from jax import lax
from jax.experimental import pallas as pl
from jax.experimental.pallas import tpu as pltpu
from jax.sharding import PartitionSpec as P

rope_theta = 1000000.0
norm_epsilon = 1e-06
masked_value = -1e30
D = 128
F32 = jnp.float32
BF16 = jnp.bfloat16
VM = pl.BlockSpec(memory_space=pltpu.VMEM)
SM = pl.BlockSpec(memory_space=pltpu.SMEM)
SCALE = D ** (-0.5)
LOG2E = math.log2(math.e)


def dot(a, b):
    return jnp.dot(a, b, preferred_element_type=F32)


def dot_rows(a, b):
    return lax.dot_general(a, b, (((1,), (1,)), ((), ())), preferred_element_type=F32)


def sin_cos(angle):
    turns = jnp.floor(angle * (2.0 / math.pi) + 0.5)
    r = angle - turns * 1.5703125
    r = r - turns * 4.837512969970703125e-4
    r = r - turns * 7.549789948768648e-8
    r2 = r * r
    s = r + r * r2 * (-1.6666654611e-1 + r2 * (8.3321608736e-3 + r2 * -1.9515295891e-4))
    c = 1.0 - 0.5 * r2 + r2 * r2 * (
        4.166664568298827e-2 + r2 * (-1.388731625493765e-3 + r2 * 2.443315711809948e-5)
    )
    quarter = turns.astype(jnp.int32)
    odd = (quarter & 1) == 1
    sin_part = jnp.where(odd, c, s)
    cos_part = jnp.where(odd, s, c)
    sin_part = jnp.where((quarter & 2) == 2, -sin_part, sin_part)
    cos_part = jnp.where(((quarter + 1) & 2) == 2, -cos_part, cos_part)
    return sin_part, cos_part


def starts_of(lengths, tokens):
    end = jnp.int32(0)
    start = jnp.zeros_like(tokens)
    for d in range(lengths.shape[1]):
        end = end + lengths[0, d]
        start = jnp.where(tokens >= end, end, start)
    return start


def unfold(table):
    turned = pltpu.roll(table, D // 2, 1)
    first_lanes = lax.broadcasted_iota(jnp.int32, table.shape, 1) < D // 2
    return jnp.where(first_lanes, table, turned), jnp.where(first_lanes, -turned, table)


def rotate(x, cosine, sine):
    return x * cosine + pltpu.roll(x, D // 2, 1) * sine


def rotate_back(x, cosine, sine):
    return x * cosine - pltpu.roll(x, D // 2, 1) * sine


def unit_of(raw):
    x = raw.astype(F32)
    inverse = lax.rsqrt(jnp.mean(x * x, axis=1, keepdims=True) + norm_epsilon)
    return x * inverse, inverse


def prep_kernel(
    heads, token_ref, lengths, freq, q_raw, dout, gain_ref,
    table_ref, table_own, q_ref, do_ref, pos_ref,
):
    tokens_own = q_raw.shape[0]
    seq = table_ref.shape[0]
    row = lax.broadcasted_iota(jnp.int32, (D, D), 0)
    lane = lax.broadcasted_iota(jnp.int32, (D, D), 1)
    tokens = row * D + lane
    positions = tokens - starts_of(lengths, tokens)
    pos_ref[...] = positions.astype(F32).T
    first_lanes = lane < D // 2
    for i in range(seq // D):
        angle = pos_ref[:, i : i + 1] * freq[...]
        s, c = sin_cos(angle)
        table_ref[i * D : (i + 1) * D, :] = jnp.where(first_lanes, c, s)
    first = pl.multiple_of(token_ref[0], tokens_own)
    mine = table_ref[pl.ds(first, tokens_own), :]
    table_own[...] = mine
    cosine, sine = unfold(mine)
    for h in range(heads):
        cols = slice(h * D, (h + 1) * D)
        rows = slice(h * tokens_own, (h + 1) * tokens_own)
        unit, _ = unit_of(q_raw[:, cols])
        q = rotate(unit * gain_ref[0:1, :], cosine, sine)
        q_ref[rows, :] = q.astype(BF16)
        do_ref[rows, :] = dout[:, cols]


def attend_kernel(
    heads, token_ref, lengths, kv_own, kv_other, table_ref, q_ref, do_ref, gain_ref,
    out_ref, dqt_buf, dkv_ref, key_sum_ref,
    s_buf, k_buf, kt_buf, vt_buf, ot_buf, max_buf, sum_buf, row_buf, kg_buf,
):
    _, tokens_own, _ = kv_own.shape
    kb = 4 * tokens_own
    blocks = kv_own.shape[0] // 2
    cols_all = heads * tokens_own
    cc = cols_all
    chunks = cols_all // cc
    first = token_ref[0]
    end = jnp.int32(0)
    low = jnp.int32(0)
    for d in range(lengths.shape[1]):
        end = end + lengths[0, d]
        low = jnp.where(end <= first, end, low)
    lo = low // kb
    hi = (first + tokens_own - 1) // kb + 1
    tok = first + lax.broadcasted_iota(jnp.int32, (8, tokens_own), 1)
    start_row = starts_of(lengths, tok)[:1]
    tok_row = tok[:1]
    dkv_ref[...] = jnp.zeros_like(dkv_ref)
    max_buf[...] = jnp.full_like(max_buf, masked_value)
    sum_buf[...] = jnp.zeros_like(sum_buf)
    ot_buf[...] = jnp.zeros_like(ot_buf)
    dqt_buf[...] = jnp.zeros_like(dqt_buf)
    kg_buf[...] = jnp.zeros_like(kg_buf)
    factor = SCALE * LOG2E

    side = (first // tokens_own) % 2

    def tables(b):
        rows = []
        for i in range(2):
            for s in (side, 1 - side):
                start = b * kb + (2 * i + s) * tokens_own
                rows.append(table_ref[pl.ds(pl.multiple_of(start, tokens_own), tokens_own), :])
        return unfold(jnp.concatenate(rows, 0))

    def keys_of(b):
        return jnp.concatenate([kv_own[2 * b, :, :D], kv_other[2 * b, :, :D], kv_own[2 * b + 1, :, :D], kv_other[2 * b + 1, :, :D]], 0)

    def values_of(b):
        return jnp.concatenate([kv_own[2 * b, :, D:], kv_other[2 * b, :, D:], kv_own[2 * b + 1, :, D:], kv_other[2 * b + 1, :, D:]], 0)

    row = lax.broadcasted_iota(jnp.int32, (kb, tokens_own), 0)
    key_shift = row + jnp.where(row % (2 * tokens_own) < tokens_own, side * tokens_own, -side * tokens_own)

    def prepare(b):
        unit, _ = unit_of(keys_of(b))
        k = rotate(unit * gain_ref[1:2, :], *tables(b))
        k_buf[b] = k.astype(BF16)
        kt_buf[b] = k.T.astype(BF16)
        vt_buf[b] = values_of(b).astype(F32).T.astype(BF16)

    def scores_step(b, carry):
        key = b * kb + key_shift
        allowed = (key >= start_row) & (key <= tok_row)
        bias = jnp.where(allowed, 0.0, masked_value)
        for c in range(chunks):
            cs = slice(c * cc, (c + 1) * cc)
            s = dot_rows(k_buf[b], q_ref[cs, :]) * factor + jnp.concatenate([bias] * (cc // tokens_own), 1)
            s_buf[b, :, cs] = s
            max_buf[:, cs] = jnp.maximum(max_buf[:, cs], jnp.max(s.reshape(kb // 8, 8, cc), axis=0))
        prepare(jnp.minimum(b + 1, blocks - 1))
        return carry

    prepare(lo)
    lax.fori_loop(lo, hi, scores_step, 0)
    row_buf[:1, :] = jnp.max(max_buf[...], axis=0, keepdims=True)

    def exp_step(b, carry):
        for c in range(chunks):
            cs = slice(c * cc, (c + 1) * cc)
            e = jnp.exp2(s_buf[b, :, cs] - row_buf[:1, cs])
            s_buf[b, :, cs] = e
            sum_buf[:, cs] += jnp.sum(e.reshape(kb // 8, 8, cc), axis=0)
            ot_buf[:, cs] += dot(vt_buf[b], e.astype(BF16))
        return carry

    lax.fori_loop(lo, hi, exp_step, 0)
    sum_buf[:1, :] = 1.0 / jnp.sum(sum_buf[...], axis=0, keepdims=True)
    for h in range(heads):
        hs = slice(h * tokens_own, (h + 1) * tokens_own)
        ot = (ot_buf[:, hs] * sum_buf[:1, hs]).astype(BF16).astype(F32)
        out_ref[:, h * D : (h + 1) * D] = ot.T.astype(BF16)
        row_buf[:1, hs] = jnp.sum(ot * do_ref[hs, :].T.astype(F32), axis=0, keepdims=True)

    def back_step(b, carry):
        dk = jnp.zeros((kb, D), F32)
        dv = jnp.zeros((kb, D), F32)
        v_rows = values_of(b)
        for c in range(chunks):
            cs = slice(c * cc, (c + 1) * cc)
            dp = dot_rows(v_rows, do_ref[cs, :])
            prob = s_buf[b, :, cs] * sum_buf[:1, cs]
            dv = dv + dot(prob.astype(BF16), do_ref[cs, :])
            ds = (prob * (dp - row_buf[:1, cs])).astype(BF16)
            dk = dk + dot(ds, q_ref[cs, :])
            dqt_buf[:, cs] += dot(kt_buf[b], ds)
        dk = dk * SCALE
        for i in range(2):
            half = slice(i * 2 * tokens_own, (i + 1) * 2 * tokens_own)
            dkv_ref[2 * b + i, :, :D] = dk[half].astype(BF16)
            dkv_ref[2 * b + i, :, D:] = dv[half].astype(BF16)
        unit, _ = unit_of(keys_of(b))
        terms = rotate_back(dk, *tables(b)) * unit
        kg_buf[...] += jnp.sum(terms.reshape(kb // 8, 8, D), axis=0)
        return carry

    lax.fori_loop(lo, hi, back_step, 0)
    key_sum_ref[...] = kg_buf[...]


def query_kernel(heads, dqt_ref, key_sum_ref, table_own, q_raw, gain_ref, dq_ref, gains_ref):
    tokens_own = q_raw.shape[0]
    cosine, sine = unfold(table_own[...])
    q_sum = jnp.zeros((8, D), F32)
    for h in range(heads):
        hs = slice(h * tokens_own, (h + 1) * tokens_own)
        back = rotate_back(dqt_ref[:, hs].T * SCALE, cosine, sine)
        unit, inverse = unit_of(q_raw[:, h * D : (h + 1) * D])
        q_sum = q_sum + jnp.sum((back * unit).reshape(tokens_own // 8, 8, D), axis=0)
        scaled = back * gain_ref[0:1, :]
        mean = jnp.mean(scaled * unit, axis=1, keepdims=True)
        dq_ref[:, h * D : (h + 1) * D] = (inverse * (scaled - unit * mean)).astype(BF16)
    gains_ref[:, :D] = jnp.broadcast_to(jnp.sum(q_sum, axis=0, keepdims=True), (8, D))
    gains_ref[:, D:] = jnp.broadcast_to(jnp.sum(key_sum_ref[...], axis=0, keepdims=True), (8, D))


def copies_kernel(*refs):
    out_ref = refs[-1]
    rows = jnp.concatenate([ref[...] for ref in refs[:-1]], axis=1)
    for i in range(out_ref.shape[0]):
        out_ref[i] = rows


def finish_kernel(own_ref, other_ref, k_raw, gain_ref, table_own, dk_ref, dv_ref):
    total = own_ref[...] + other_ref[...].astype(F32)
    unit, inverse = unit_of(k_raw[...])
    back = rotate_back(total[:, :D], *unfold(table_own[...]))
    scaled = back * gain_ref[1:2, :]
    mean = jnp.mean(scaled * unit, axis=1, keepdims=True)
    dk_ref[...] = (inverse * (scaled - unit * mean)).astype(BF16)
    dv_ref[...] = total[:, D:].astype(BF16)


def call_prep(token, lengths, freq, q_raw, dout, both_gains, seq, **kw):
    tokens_own, width = q_raw.shape
    heads = width // D
    rows = heads * tokens_own
    shapes = [
        ((seq, D), F32), ((tokens_own, D), F32),
        ((rows, D), BF16), ((rows, D), BF16),
    ]
    return pl.pallas_call(
        functools.partial(prep_kernel, heads),
        out_shape=[jax.ShapeDtypeStruct(s, t) for s, t in shapes],
        in_specs=[SM, SM, VM, VM, VM, VM],
        out_specs=[VM] * len(shapes),
        scratch_shapes=[pltpu.VMEM((D, D), F32)],
        compiler_params=pltpu.CompilerParams(vmem_limit_bytes=12 * 2**20),
        cost_estimate=pl.CostEstimate(flops=40_000_000, bytes_accessed=4_000_000, transcendentals=0),
        name="prep",
        **kw,
    )(token, lengths, freq, q_raw, dout, both_gains)


def call_attend(token, lengths, kv_own, kv_other, table, q_rows, do_rows, both_gains, **kw):
    tokens_own = kv_own.shape[1]
    heads = q_rows.shape[0] // tokens_own
    width = heads * D
    blocks = kv_own.shape[0] // 2
    kb = 4 * tokens_own
    rows = heads * tokens_own
    shapes = [
        ((tokens_own, width), BF16), ((D, rows), F32), ((2 * blocks, kb // 2, 2 * D), BF16), ((8, D), F32),
    ]
    scratch = [
        pltpu.VMEM((blocks, kb, rows), F32),
        pltpu.VMEM((blocks, kb, D), BF16), pltpu.VMEM((blocks, D, kb), BF16),
        pltpu.VMEM((blocks, D, kb), BF16), pltpu.VMEM((D, rows), F32),
        pltpu.VMEM((8, rows), F32), pltpu.VMEM((8, rows), F32), pltpu.VMEM((8, rows), F32),
        pltpu.VMEM((8, D), F32),
    ]
    return pl.pallas_call(
        functools.partial(attend_kernel, heads),
        out_shape=[jax.ShapeDtypeStruct(s, t) for s, t in shapes],
        in_specs=[SM, SM] + [VM] * 6,
        out_specs=[VM] * len(shapes),
        scratch_shapes=scratch,
        compiler_params=pltpu.CompilerParams(vmem_limit_bytes=20 * 2**20),
        cost_estimate=pl.CostEstimate(flops=3_200_000_000, bytes_accessed=8_000_000, transcendentals=2_000_000),
        name="attend",
        **kw,
    )(token, lengths, kv_own, kv_other, table, q_rows, do_rows, both_gains)


def call_copies(count, *parts):
    shape = (count, parts[0].shape[0], sum(part.shape[1] for part in parts))
    size = math.prod(shape) * parts[0].dtype.itemsize
    return pl.pallas_call(
        copies_kernel,
        out_shape=jax.ShapeDtypeStruct(shape, parts[0].dtype),
        in_specs=[VM] * len(parts),
        out_specs=VM,
        compiler_params=pltpu.CompilerParams(vmem_limit_bytes=4 * 2**20),
        cost_estimate=pl.CostEstimate(flops=0, bytes_accessed=size, transcendentals=0),
        name="copies",
    )(*parts)


def call_query(dqt, key_sum, table_own, q_raw, both_gains, **kw):
    heads = q_raw.shape[1] // D
    return pl.pallas_call(
        functools.partial(query_kernel, heads),
        out_shape=[jax.ShapeDtypeStruct(q_raw.shape, BF16), jax.ShapeDtypeStruct((8, 2 * D), F32)],
        in_specs=[VM] * 5,
        out_specs=[VM] * 2,
        compiler_params=pltpu.CompilerParams(vmem_limit_bytes=12 * 2**20),
        cost_estimate=pl.CostEstimate(flops=5_000_000, bytes_accessed=2_000_000, transcendentals=0),
        name="query",
        **kw,
    )(dqt, key_sum, table_own, q_raw, both_gains)


def call_finish(own, other, k_raw, both_gains, table_own, **kw):
    shape = jax.ShapeDtypeStruct(k_raw.shape, BF16)
    return pl.pallas_call(
        finish_kernel,
        out_shape=[shape, shape],
        in_specs=[VM] * 5,
        out_specs=[VM] * 2,
        compiler_params=pltpu.CompilerParams(vmem_limit_bytes=4 * 2**20),
        cost_estimate=pl.CostEstimate(flops=1_000_000, bytes_accessed=500_000, transcendentals=0),
        name="finish",
        **kw,
    )(own, other, k_raw, both_gains, table_own)


def frequency_row():
    exponent = jnp.arange(D // 2, dtype=F32) * (2.0 / D)
    frequency = jnp.power(F32(rope_theta), -exponent)
    return jnp.concatenate([frequency, frequency])[None, :]


def strided(size, stride, count):
    span = stride * count
    return [
        [base + low + stride * k for k in range(count)]
        for base in range(0, size, span)
        for low in range(stride)
    ]


def body(query_raw, key_raw, values, out_grad, doc_lengths, query_gain, key_gain):
    tokens_own = query_raw.shape[1]
    ctx = lax.axis_size("ctx")
    dp = lax.axis_size("dp")
    seq = tokens_own * ctx
    half = ctx // 2
    me = lax.axis_index("ctx")
    token = (me * tokens_own)[None].astype(jnp.int32)
    both_gains = jnp.stack([query_gain, key_gain] * 4)
    columns = [[2 * y + z for y in range(half)] for z in range(2)]
    swap = [(i, i ^ 1) for i in range(ctx)]

    def exchange(blocks):
        return lax.all_to_all(blocks, "ctx", 0, 0, axis_index_groups=columns)

    def spread(rows):
        return jnp.broadcast_to(rows[None], (half,) + rows.shape)

    kv = jnp.concatenate([key_raw[0], values[0]], axis=1)
    kv_swapped = lax.ppermute(kv, "ctx", swap)
    kv_own = exchange(
        jnp.concatenate([spread(key_raw[0]), spread(values[0])], axis=2)
    )
    kv_other = exchange(call_copies(half, kv_swapped))
    table, table_own, q_rows, do_rows = call_prep(token, doc_lengths, frequency_row(), query_raw[0], out_grad[0], both_gains, seq)
    output, dqt, parts, key_sum = call_attend(
        token, doc_lengths, kv_own, kv_other, table, q_rows, do_rows, both_gains
    )
    received = exchange(parts)
    dq, gains = call_query(dqt, key_sum, table_own, query_raw[0], both_gains)
    own = jnp.sum(received[:, :tokens_own].astype(F32), axis=0)
    theirs = jnp.sum(received[:, tokens_own:].astype(F32), axis=0).astype(BF16)
    def flat(x, y, z, core):
        return ((x * 4 + z % 4) * 2 + core) * ctx + 2 * y + z // 4

    xs, ys, zs, cores = range(dp // 8), range(half), range(8), range(2)
    along_z = [[flat(x, y, z, core) for z in zs] for x in xs for y in ys for core in cores]
    along_y = [[flat(x, y, z, core) for y in ys for core in cores] for x in xs for z in zs]
    gains = lax.psum(gains[0], "dp", axis_index_groups=strided(dp, 8, dp // 8))
    gains = lax.psum(gains, ("dp", "ctx"), axis_index_groups=along_z)
    copies = call_copies(len(along_y[0]), gains[None])
    theirs, copies = lax.optimization_barrier((theirs, copies))
    other = lax.ppermute(theirs, "ctx", swap)
    gains = lax.all_to_all(copies, ("dp", "ctx"), 0, 0, axis_index_groups=along_y)
    gains = jnp.sum(gains, axis=(0, 1))
    dk, dv = call_finish(own, other, key_raw[0], both_gains, table_own)
    return (output[None], dq[None], dk[None], dv[None], gains[:D], gains[D:])


def solution(mesh):
    return jax.shard_map(
        body,
        mesh=mesh,
        in_specs=(
            P("dp", "ctx", None),
            P("dp", "ctx", None),
            P("dp", "ctx", None),
            P("dp", "ctx", None),
            P("dp", None),
            P(),
            P(),
        ),
        out_specs=(
            P("dp", "ctx", None),
            P("dp", "ctx", None),
            P("dp", "ctx", None),
            P("dp", "ctx", None),
            P(),
            P(),
        ),
        check_vma=False,
    )
```

```python
import functools
import math

import jax
import jax.numpy as jnp
from jax import lax
from jax.experimental import pallas as pl
from jax.experimental.pallas import tpu as pltpu
from jax.sharding import PartitionSpec as P

rope_theta = 1000000.0
norm_epsilon = 1e-06
masked_value = -1e30
D = 128
F32 = jnp.float32
BF16 = jnp.bfloat16
VM = pl.BlockSpec(memory_space=pltpu.VMEM)
SM = pl.BlockSpec(memory_space=pltpu.SMEM)
SCALE = D ** (-0.5)
LOG2E = math.log2(math.e)


def dot(a, b):
    return jnp.dot(a, b, preferred_element_type=F32)


def dot_rows(a, b):
    return lax.dot_general(a, b, (((1,), (1,)), ((), ())), preferred_element_type=F32)


def sin_cos(angle):
    turns = jnp.floor(angle * (2.0 / math.pi) + 0.5)
    r = angle - turns * 1.5703125
    r = r - turns * 4.837512969970703125e-4
    r = r - turns * 7.549789948768648e-8
    r2 = r * r
    s = r + r * r2 * (-1.6666654611e-1 + r2 * (8.3321608736e-3 + r2 * -1.9515295891e-4))
    c = 1.0 - 0.5 * r2 + r2 * r2 * (
        4.166664568298827e-2 + r2 * (-1.388731625493765e-3 + r2 * 2.443315711809948e-5)
    )
    quarter = turns.astype(jnp.int32)
    odd = (quarter & 1) == 1
    sin_part = jnp.where(odd, c, s)
    cos_part = jnp.where(odd, s, c)
    sin_part = jnp.where((quarter & 2) == 2, -sin_part, sin_part)
    cos_part = jnp.where(((quarter + 1) & 2) == 2, -cos_part, cos_part)
    return sin_part, cos_part


def starts_of(lengths, tokens):
    end = jnp.int32(0)
    start = jnp.zeros_like(tokens)
    for d in range(lengths.shape[1]):
        end = end + lengths[0, d]
        start = jnp.where(tokens >= end, end, start)
    return start


def unfold(table):
    turned = pltpu.roll(table, D // 2, 1)
    first_lanes = lax.broadcasted_iota(jnp.int32, table.shape, 1) < D // 2
    return jnp.where(first_lanes, table, turned), jnp.where(first_lanes, -turned, table)


def rotate(x, cosine, sine):
    return x * cosine + pltpu.roll(x, D // 2, 1) * sine


def rotate_back(x, cosine, sine):
    return x * cosine - pltpu.roll(x, D // 2, 1) * sine


def unit_of(raw):
    x = raw.astype(F32)
    inverse = lax.rsqrt(jnp.mean(x * x, axis=1, keepdims=True) + norm_epsilon)
    return x * inverse, inverse


def prep_kernel(
    heads, token_ref, lengths, freq, q_raw, dout, gain_ref,
    table_ref, table_own, q_ref, do_ref, pos_ref,
):
    tokens_own = q_raw.shape[0]
    seq = table_ref.shape[0]
    row = lax.broadcasted_iota(jnp.int32, (D, D), 0)
    lane = lax.broadcasted_iota(jnp.int32, (D, D), 1)
    tokens = row * D + lane
    positions = tokens - starts_of(lengths, tokens)
    pos_ref[...] = positions.astype(F32).T
    first_lanes = lane < D // 2
    for i in range(seq // D):
        angle = pos_ref[:, i : i + 1] * freq[...]
        s, c = sin_cos(angle)
        table_ref[i * D : (i + 1) * D, :] = jnp.where(first_lanes, c, s)
    first = pl.multiple_of(token_ref[0], tokens_own)
    mine = table_ref[pl.ds(first, tokens_own), :]
    table_own[...] = mine
    cosine, sine = unfold(mine)
    for h in range(heads):
        cols = slice(h * D, (h + 1) * D)
        rows = slice(h * tokens_own, (h + 1) * tokens_own)
        unit, _ = unit_of(q_raw[:, cols])
        q = rotate(unit * gain_ref[0:1, :], cosine, sine)
        q_ref[rows, :] = q.astype(BF16)
        do_ref[rows, :] = dout[:, cols]


def attend_kernel(
    heads, token_ref, lengths, kv_own, kv_other, table_ref, q_ref, do_ref, gain_ref,
    out_ref, dqt_buf, dkv_ref, key_sum_ref,
    s_buf, k_buf, kt_buf, vt_buf, ot_buf, max_buf, sum_buf, row_buf, kg_buf,
):
    _, tokens_own, _ = kv_own.shape
    kb = 4 * tokens_own
    blocks = kv_own.shape[0] // 2
    cols_all = heads * tokens_own
    cc = cols_all
    chunks = cols_all // cc
    first = token_ref[0]
    end = jnp.int32(0)
    low = jnp.int32(0)
    for d in range(lengths.shape[1]):
        end = end + lengths[0, d]
        low = jnp.where(end <= first, end, low)
    lo = low // kb
    hi = (first + tokens_own - 1) // kb + 1
    tok = first + lax.broadcasted_iota(jnp.int32, (8, tokens_own), 1)
    start_row = starts_of(lengths, tok)[:1]
    tok_row = tok[:1]
    for i in range(2 * blocks):

        @pl.when((i // 2 < lo) | (i // 2 >= hi))
        def _():
            dkv_ref[i] = jnp.zeros(dkv_ref.shape[1:], BF16)

    max_buf[...] = jnp.full_like(max_buf, masked_value)
    sum_buf[...] = jnp.zeros_like(sum_buf)
    ot_buf[...] = jnp.zeros_like(ot_buf)
    dqt_buf[...] = jnp.zeros_like(dqt_buf)
    kg_buf[...] = jnp.zeros_like(kg_buf)
    factor = SCALE * LOG2E

    side = (first // tokens_own) % 2

    def tables(b):
        rows = []
        for i in range(2):
            for s in (side, 1 - side):
                start = b * kb + (2 * i + s) * tokens_own
                rows.append(table_ref[pl.ds(pl.multiple_of(start, tokens_own), tokens_own), :])
        return unfold(jnp.concatenate(rows, 0))

    def keys_of(b):
        return jnp.concatenate([kv_own[2 * b, :, :D], kv_other[2 * b, :, :D], kv_own[2 * b + 1, :, :D], kv_other[2 * b + 1, :, :D]], 0)

    def values_of(b):
        return jnp.concatenate([kv_own[2 * b, :, D:], kv_other[2 * b, :, D:], kv_own[2 * b + 1, :, D:], kv_other[2 * b + 1, :, D:]], 0)

    row = lax.broadcasted_iota(jnp.int32, (kb, tokens_own), 0)
    key_shift = row + jnp.where(row % (2 * tokens_own) < tokens_own, side * tokens_own, -side * tokens_own)

    def prepare(b):
        unit, _ = unit_of(keys_of(b))
        k = rotate(unit * gain_ref[1:2, :], *tables(b))
        k_buf[b] = k.astype(BF16)
        kt_buf[b] = k.T.astype(BF16)
        vt_buf[b] = values_of(b).astype(F32).T.astype(BF16)

    def scores_step(b, carry):
        key = b * kb + key_shift
        allowed = (key >= start_row) & (key <= tok_row)
        bias = jnp.where(allowed, 0.0, masked_value)
        for c in range(chunks):
            cs = slice(c * cc, (c + 1) * cc)
            s = dot_rows(k_buf[b], q_ref[cs, :]) * factor + jnp.concatenate([bias] * (cc // tokens_own), 1)
            s_buf[b, :, cs] = s
            max_buf[:, cs] = jnp.maximum(max_buf[:, cs], jnp.max(s.reshape(kb // 8, 8, cc), axis=0))
        prepare(jnp.minimum(b + 1, blocks - 1))
        return carry

    prepare(lo)
    lax.fori_loop(lo, hi, scores_step, 0)
    row_buf[:1, :] = jnp.max(max_buf[...], axis=0, keepdims=True)

    def exp_step(b, carry):
        for c in range(chunks):
            cs = slice(c * cc, (c + 1) * cc)
            e = jnp.exp2(s_buf[b, :, cs] - row_buf[:1, cs])
            s_buf[b, :, cs] = e
            sum_buf[:, cs] += jnp.sum(e.reshape(kb // 8, 8, cc), axis=0)
            ot_buf[:, cs] += dot(vt_buf[b], e.astype(BF16))
        return carry

    lax.fori_loop(lo, hi, exp_step, 0)
    sum_buf[:1, :] = 1.0 / jnp.sum(sum_buf[...], axis=0, keepdims=True)
    for h in range(heads):
        hs = slice(h * tokens_own, (h + 1) * tokens_own)
        ot = (ot_buf[:, hs] * sum_buf[:1, hs]).astype(BF16).astype(F32)
        out_ref[:, h * D : (h + 1) * D] = ot.T.astype(BF16)
        row_buf[:1, hs] = jnp.sum(ot * do_ref[hs, :].T.astype(F32), axis=0, keepdims=True)

    def back_step(b, carry):
        dk = jnp.zeros((kb, D), F32)
        dv = jnp.zeros((kb, D), F32)
        v_rows = values_of(b)
        for c in range(chunks):
            cs = slice(c * cc, (c + 1) * cc)
            dp = dot_rows(v_rows, do_ref[cs, :])
            prob = s_buf[b, :, cs] * sum_buf[:1, cs]
            dv = dv + dot(prob.astype(BF16), do_ref[cs, :])
            ds = (prob * (dp - row_buf[:1, cs])).astype(BF16)
            dk = dk + dot(ds, q_ref[cs, :])
            dqt_buf[:, cs] += dot(kt_buf[b], ds)
        dk = dk * SCALE
        for i in range(2):
            half = slice(i * 2 * tokens_own, (i + 1) * 2 * tokens_own)
            dkv_ref[2 * b + i, :, :D] = dk[half].astype(BF16)
            dkv_ref[2 * b + i, :, D:] = dv[half].astype(BF16)
        unit, _ = unit_of(keys_of(b))
        terms = rotate_back(dk, *tables(b)) * unit
        kg_buf[...] += jnp.sum(terms.reshape(kb // 8, 8, D), axis=0)
        return carry

    lax.fori_loop(lo, hi, back_step, 0)
    key_sum_ref[...] = kg_buf[...]


def query_kernel(heads, dqt_ref, key_sum_ref, table_own, q_raw, gain_ref, dq_ref, gains_ref):
    tokens_own = q_raw.shape[0]
    cosine, sine = unfold(table_own[...])
    q_sum = jnp.zeros((8, D), F32)
    for h in range(heads):
        hs = slice(h * tokens_own, (h + 1) * tokens_own)
        back = rotate_back(dqt_ref[:, hs].T * SCALE, cosine, sine)
        unit, inverse = unit_of(q_raw[:, h * D : (h + 1) * D])
        q_sum = q_sum + jnp.sum((back * unit).reshape(tokens_own // 8, 8, D), axis=0)
        scaled = back * gain_ref[0:1, :]
        mean = jnp.mean(scaled * unit, axis=1, keepdims=True)
        dq_ref[:, h * D : (h + 1) * D] = (inverse * (scaled - unit * mean)).astype(BF16)
    gains_ref[:, :D] = jnp.broadcast_to(jnp.sum(q_sum, axis=0, keepdims=True), (8, D))
    gains_ref[:, D:] = jnp.broadcast_to(jnp.sum(key_sum_ref[...], axis=0, keepdims=True), (8, D))


def copies_kernel(*refs):
    out_ref = refs[-1]
    rows = jnp.concatenate([ref[...] for ref in refs[:-1]], axis=1)
    for i in range(out_ref.shape[0]):
        out_ref[i] = rows


def finish_kernel(own_ref, other_ref, k_raw, gain_ref, table_own, dk_ref, dv_ref):
    total = own_ref[...] + other_ref[...].astype(F32)
    unit, inverse = unit_of(k_raw[...])
    back = rotate_back(total[:, :D], *unfold(table_own[...]))
    scaled = back * gain_ref[1:2, :]
    mean = jnp.mean(scaled * unit, axis=1, keepdims=True)
    dk_ref[...] = (inverse * (scaled - unit * mean)).astype(BF16)
    dv_ref[...] = total[:, D:].astype(BF16)


def call_prep(token, lengths, freq, q_raw, dout, both_gains, seq, **kw):
    tokens_own, width = q_raw.shape
    heads = width // D
    rows = heads * tokens_own
    shapes = [
        ((seq, D), F32), ((tokens_own, D), F32),
        ((rows, D), BF16), ((rows, D), BF16),
    ]
    return pl.pallas_call(
        functools.partial(prep_kernel, heads),
        out_shape=[jax.ShapeDtypeStruct(s, t) for s, t in shapes],
        in_specs=[SM, SM, VM, VM, VM, VM],
        out_specs=[VM] * len(shapes),
        scratch_shapes=[pltpu.VMEM((D, D), F32)],
        compiler_params=pltpu.CompilerParams(vmem_limit_bytes=12 * 2**20),
        cost_estimate=pl.CostEstimate(flops=40_000_000, bytes_accessed=4_000_000, transcendentals=0),
        name="prep",
        **kw,
    )(token, lengths, freq, q_raw, dout, both_gains)


def call_attend(token, lengths, kv_own, kv_other, table, q_rows, do_rows, both_gains, **kw):
    tokens_own = kv_own.shape[1]
    heads = q_rows.shape[0] // tokens_own
    width = heads * D
    blocks = kv_own.shape[0] // 2
    kb = 4 * tokens_own
    rows = heads * tokens_own
    shapes = [
        ((tokens_own, width), BF16), ((D, rows), F32), ((2 * blocks, kb // 2, 2 * D), BF16), ((8, D), F32),
    ]
    scratch = [
        pltpu.VMEM((blocks, kb, rows), F32),
        pltpu.VMEM((blocks, kb, D), BF16), pltpu.VMEM((blocks, D, kb), BF16),
        pltpu.VMEM((blocks, D, kb), BF16), pltpu.VMEM((D, rows), F32),
        pltpu.VMEM((8, rows), F32), pltpu.VMEM((8, rows), F32), pltpu.VMEM((8, rows), F32),
        pltpu.VMEM((8, D), F32),
    ]
    return pl.pallas_call(
        functools.partial(attend_kernel, heads),
        out_shape=[jax.ShapeDtypeStruct(s, t) for s, t in shapes],
        in_specs=[SM, SM] + [VM] * 6,
        out_specs=[VM] * len(shapes),
        scratch_shapes=scratch,
        compiler_params=pltpu.CompilerParams(vmem_limit_bytes=20 * 2**20),
        cost_estimate=pl.CostEstimate(flops=3_200_000_000, bytes_accessed=8_000_000, transcendentals=2_000_000),
        name="attend",
        **kw,
    )(token, lengths, kv_own, kv_other, table, q_rows, do_rows, both_gains)


def call_copies(count, *parts):
    shape = (count, parts[0].shape[0], sum(part.shape[1] for part in parts))
    size = math.prod(shape) * parts[0].dtype.itemsize
    return pl.pallas_call(
        copies_kernel,
        out_shape=jax.ShapeDtypeStruct(shape, parts[0].dtype),
        in_specs=[VM] * len(parts),
        out_specs=VM,
        compiler_params=pltpu.CompilerParams(vmem_limit_bytes=4 * 2**20),
        cost_estimate=pl.CostEstimate(flops=0, bytes_accessed=size, transcendentals=0),
        name="copies",
    )(*parts)


def call_query(dqt, key_sum, table_own, q_raw, both_gains, **kw):
    heads = q_raw.shape[1] // D
    return pl.pallas_call(
        functools.partial(query_kernel, heads),
        out_shape=[jax.ShapeDtypeStruct(q_raw.shape, BF16), jax.ShapeDtypeStruct((8, 2 * D), F32)],
        in_specs=[VM] * 5,
        out_specs=[VM] * 2,
        compiler_params=pltpu.CompilerParams(vmem_limit_bytes=12 * 2**20),
        cost_estimate=pl.CostEstimate(flops=5_000_000, bytes_accessed=2_000_000, transcendentals=0),
        name="query",
        **kw,
    )(dqt, key_sum, table_own, q_raw, both_gains)


def call_finish(own, other, k_raw, both_gains, table_own, **kw):
    shape = jax.ShapeDtypeStruct(k_raw.shape, BF16)
    return pl.pallas_call(
        finish_kernel,
        out_shape=[shape, shape],
        in_specs=[VM] * 5,
        out_specs=[VM] * 2,
        compiler_params=pltpu.CompilerParams(vmem_limit_bytes=4 * 2**20),
        cost_estimate=pl.CostEstimate(flops=1_000_000, bytes_accessed=500_000, transcendentals=0),
        name="finish",
        **kw,
    )(own, other, k_raw, both_gains, table_own)


def frequency_row():
    exponent = jnp.arange(D // 2, dtype=F32) * (2.0 / D)
    frequency = jnp.power(F32(rope_theta), -exponent)
    return jnp.concatenate([frequency, frequency])[None, :]


def strided(size, stride, count):
    span = stride * count
    return [
        [base + low + stride * k for k in range(count)]
        for base in range(0, size, span)
        for low in range(stride)
    ]


def body(query_raw, key_raw, values, out_grad, doc_lengths, query_gain, key_gain):
    tokens_own = query_raw.shape[1]
    ctx = lax.axis_size("ctx")
    dp = lax.axis_size("dp")
    seq = tokens_own * ctx
    half = ctx // 2
    me = lax.axis_index("ctx")
    token = (me * tokens_own)[None].astype(jnp.int32)
    both_gains = jnp.stack([query_gain, key_gain] * 4)
    columns = [[2 * y + z for y in range(half)] for z in range(2)]
    swap = [(i, i ^ 1) for i in range(ctx)]

    def exchange(blocks):
        return lax.all_to_all(blocks, "ctx", 0, 0, axis_index_groups=columns)

    def spread(rows):
        return jnp.broadcast_to(rows[None], (half,) + rows.shape)

    kv = jnp.concatenate([key_raw[0], values[0]], axis=1)
    kv_swapped = lax.ppermute(kv, "ctx", swap)
    kv_own = exchange(
        jnp.concatenate([spread(key_raw[0]), spread(values[0])], axis=2)
    )
    kv_other = exchange(call_copies(half, kv_swapped))
    table, table_own, q_rows, do_rows = call_prep(token, doc_lengths, frequency_row(), query_raw[0], out_grad[0], both_gains, seq)
    output, dqt, parts, key_sum = call_attend(
        token, doc_lengths, kv_own, kv_other, table, q_rows, do_rows, both_gains
    )
    received = exchange(parts)
    dq, gains = call_query(dqt, key_sum, table_own, query_raw[0], both_gains)
    own = jnp.sum(received[:, :tokens_own].astype(F32), axis=0)
    theirs = jnp.sum(received[:, tokens_own:].astype(F32), axis=0).astype(BF16)
    def flat(x, y, z, core):
        return ((x * 4 + z % 4) * 2 + core) * ctx + 2 * y + z // 4

    xs, ys, zs, cores = range(dp // 8), range(half), range(8), range(2)
    along_z = [[flat(x, y, z, core) for z in zs] for x in xs for y in ys for core in cores]
    along_xy = [[flat(x, y, z, core) for x in xs for y in ys] for z in zs for core in cores]
    gains = lax.psum(gains[0], "dp", axis_index_groups=strided(dp, 1, 2))
    gains = lax.psum(gains, ("dp", "ctx"), axis_index_groups=along_z)
    copies = call_copies(len(along_xy[0]), gains[None])
    theirs, copies = lax.optimization_barrier((theirs, copies))
    other = lax.ppermute(theirs, "ctx", swap)
    gains = lax.all_to_all(copies, ("dp", "ctx"), 0, 0, axis_index_groups=along_xy)
    gains = jnp.sum(gains, axis=(0, 1))
    dk, dv = call_finish(own, other, key_raw[0], both_gains, table_own)
    return (output[None], dq[None], dk[None], dv[None], gains[:D], gains[D:])


def solution(mesh):
    return jax.shard_map(
        body,
        mesh=mesh,
        in_specs=(
            P("dp", "ctx", None),
            P("dp", "ctx", None),
            P("dp", "ctx", None),
            P("dp", "ctx", None),
            P("dp", None),
            P(),
            P(),
        ),
        out_specs=(
            P("dp", "ctx", None),
            P("dp", "ctx", None),
            P("dp", "ctx", None),
            P("dp", "ctx", None),
            P(),
            P(),
        ),
        check_vma=False,
    )
```
